128 devices in a mesh: dp: 16 (over y, z_hi, core), seq: 8 (over x, z_lo).
Axes of the slice: x: 4, y: 4, z: 4 (z_hi: 2, z_lo: 2; z = z_hi * 2 + z_lo), core: 2. Of those that a mesh axis runs over, the one named last changes fastest.
Arguments:
- inputs: bfloat16 [16, 1024, 1024], P('dp', 'seq'), may hold values from -6 to 6
- cotangent: bfloat16 [16, 1024, 1024], P('dp', 'seq'), may hold values from -6 to 6
- mixer_in: bfloat16 [1, 1024, 3352], P(None, 'seq'), may hold values from -0.1875 to 0.1875
- attn_in: bfloat16 [1, 1024, 768], P(None, 'seq'), may hold values from -0.1875 to 0.1875
- mamba_out: bfloat16 [1, 1536, 1024], P(None, 'seq'), may hold values from -0.15625 to 0.15625
- attn_out: bfloat16 [1, 512, 1024], P(None, 'seq'), may hold values from -1 to 1
- gate_up: bfloat16 [1, 1024, 4096], P(None, 'seq'), may hold values from -0.1875 to 0.1875
- down_proj: bfloat16 [1, 2048, 1024], P(None, 'seq'), may hold values from -0.125 to 0.125
- norm_gains: bfloat16 [1, 2, 1024], P(None, None, 'seq'), may hold values from 0.5 to 1.5
- step_bias: bfloat16 [1, 24], P(None, 'seq'), may hold values from -6 to -3
- decay_log: bfloat16 [1, 24], P(None, 'seq'), may hold values from 0 to 2.5
- skip_gain: bfloat16 [1, 24], P(None, 'seq'), may hold values from 0.5 to 1.5
Outputs:
- outputs: bfloat16 [16, 1024, 1024], P('dp', 'seq')
- input_grad: float32 [16, 1024, 1024], P('dp', 'seq')
- mixer_in_grad: float32 [1, 1024, 3352], P(None, 'seq')
- attn_in_grad: float32 [1, 1024, 768], P(None, 'seq')
- mamba_out_grad: float32 [1, 1536, 1024], P(None, 'seq')
- attn_out_grad: float32 [1, 512, 1024], P(None, 'seq')
- gate_up_grad: float32 [1, 1024, 4096], P(None, 'seq')
- down_proj_grad: float32 [1, 2048, 1024], P(None, 'seq')
- norm_gains_grad: float32 [1, 2, 1024], P(None, None, 'seq')
- step_bias_grad: float32 [1, 24], P(None, 'seq')
- decay_log_grad: float32 [1, 24], P(None, 'seq')
- skip_gain_grad: float32 [1, 24], P(None, 'seq')
The draws below stay inside these ranges and needn't reach their ends.
All inputs are finite; a program needn't handle non-finite values.
Results may differ from the reference program's by a relative error of at most 0.03.
Values may be sent and summed in bfloat16 or wider, within the bound.
No kernel may reach another device: no remote copies, remote signals or barrier semaphores. Data moves between devices by JAX's collectives and lax.ppermute only.
A program may use at most 192 MiB of HBM per device.

```python
import jax
import jax.numpy as jnp
from jax import lax

D = 1024
FF = 2048
QUERY_HEADS = 8
KEY_VALUE_HEADS = 2
HEAD_SIZE = 64
MH = 24
MP = 64
NS = 128
LAYERS = 1
SPAN = 64
SEQ_LEN = 1024
SEQS = 16
PROJ = 3352
QKV = 768


def steps_of(stream_key, shape, cuts, low, top_value):
    level = 1.0
    for position, shards_of in cuts:
        heights = jax.random.uniform(jax.random.fold_in(jax.random.fold_in(stream_key, 6), position), (shards_of,), jnp.float32, low / len(cuts), top_value / len(cuts))
        level = level * jnp.repeat(jnp.exp(heights), shape[position] // shards_of).reshape((-1,) + (1,) * (len(shape) - 1 - position))
    return level


def centred(own_key, dims, width, most, cuts=(), kind=jnp.bfloat16):
    drawn = width * jax.random.normal(own_key, dims, jnp.float32)
    if cuts:
        drawn = drawn * steps_of(own_key, dims, cuts, -0.22, 0.18)
    return jnp.clip(drawn, -most, most).astype(kind)


def setup_inputs(seed: int = 0) -> dict:
    arg_keys = jax.random.split(jax.random.key(seed), 13)
    return {
        "inputs": centred(arg_keys[0], (SEQS, SEQ_LEN, D), 1.0, 6.0, ((0, 16), (1, 8))),
        "cotangent": centred(arg_keys[1], (SEQS, SEQ_LEN, D), 1.0, 6.0, ((0, 16), (1, 8))),
        "mixer_in": centred(arg_keys[2], (LAYERS, D, PROJ), D ** -0.5, 0.1875, ((1, 8),)),
        "attn_in": centred(arg_keys[3], (LAYERS, D, QKV), D ** -0.5, 0.1875, ((1, 8),)),
        "mamba_out": centred(arg_keys[4], (LAYERS, MH * MP, D), (MH * MP) ** -0.5, 0.15625, ((1, 8),)),
        "attn_out": centred(arg_keys[5], (LAYERS, QUERY_HEADS * HEAD_SIZE, D), (QUERY_HEADS * HEAD_SIZE // 16) ** -0.5, 1.0, ((1, 8),)),
        "gate_up": centred(arg_keys[6], (LAYERS, D, 2 * FF), D ** -0.5, 0.1875, ((1, 8),)),
        "down_proj": centred(arg_keys[7], (LAYERS, FF, D), FF ** -0.5, 0.125, ((1, 8),)),
        "norm_gains": jnp.clip(1.0 + 0.1 * jax.random.normal(arg_keys[8], (LAYERS, 2, D), jnp.float32), 0.5, 1.5).astype(jnp.bfloat16),
        "step_bias": jnp.clip(-6.0 + 3.0 * jax.random.uniform(arg_keys[9], (LAYERS, MH), jnp.float32) ** steps_of(arg_keys[9], (LAYERS, MH), ((1, 8),), -0.2, 0.2), -6.0, -3.0).astype(jnp.bfloat16),
        "decay_log": jnp.clip(2.5 * jax.random.uniform(arg_keys[10], (LAYERS, MH), jnp.float32) ** steps_of(arg_keys[10], (LAYERS, MH), ((1, 8),), -0.2, 0.2), 0.0, 2.5).astype(jnp.bfloat16),
        "skip_gain": jnp.clip(0.5 + 1.0 * jax.random.uniform(arg_keys[11], (LAYERS, MH), jnp.float32) ** steps_of(arg_keys[11], (LAYERS, MH), ((1, 8),), -0.2, 0.2), 0.5, 1.5).astype(jnp.bfloat16),
    }


@jax.custom_vjp
def low(v):
    return lax.optimization_barrier(v.astype(jnp.bfloat16)).astype(jnp.float32)

@jax.custom_vjp
def low_back(v):
    return v

def low_keep(v):
    return (low(v), None)

def low_pass(kept, grad):
    return (grad,)

def back_keep(v):
    return (v, None)

def back_low(kept, grad):
    return (low(grad),)
low.defvjp(low_keep, low_pass)
low_back.defvjp(back_keep, back_low)
highest = lax.Precision.HIGHEST
norm_epsilon = 1e-05
masked_score = -1e+30

def matmul_high(left, right):
    return jnp.dot(left, right, precision=highest)

def sigmoid_linear(value_rows):
    return value_rows * jax.nn.sigmoid(value_rows)

def norm_rows(value_rows, scales):
    return value_rows * lax.rsqrt(lax.optimization_barrier(jnp.mean(value_rows * value_rows, axis=-1, keepdims=True)) + norm_epsilon) * scales

def span_step(carried, pieces):
    scaled_x, log_decay, in_basis, out_basis = pieces
    cumulated = jnp.cumsum(log_decay, axis=0)
    length = log_decay.shape[0]
    causal = jnp.arange(length)[:, None] >= jnp.arange(length)[None, :]
    spread = jnp.where(causal[:, :, None], cumulated[:, None, :] - cumulated[None, :, :], masked_score)
    mixing = jnp.exp(spread) * jnp.dot(out_basis, in_basis.T, precision=highest)[:, :, None]
    result = jnp.einsum('tsh,shp->thp', mixing, scaled_x, precision=highest)
    result = result + jnp.exp(cumulated)[:, :, None] * jnp.einsum('tn,hpn->thp', out_basis, carried, precision=highest)
    final_cumul = cumulated[-1]
    weight_in = jnp.exp(final_cumul[None, :] - cumulated)
    new_state = jnp.exp(final_cumul)[:, None, None] * carried + jnp.einsum('sh,shp,sn->hpn', weight_in, scaled_x, in_basis, precision=highest)
    return (new_state, result)

def mamba_mix(gate_raw, inner_x, in_basis, out_basis, step_raw, step_shift, decay_rate, skip_weight):
    count_of_rows = inner_x.shape[0]
    step_size = jnp.log1p(jnp.exp(step_raw + step_shift))
    log_decay = -jnp.exp(decay_rate) * step_size
    per_head = inner_x.reshape(count_of_rows, MH, MP)
    scaled_x = per_head * step_size[:, :, None]
    block_count = count_of_rows // SPAN
    pieces = (scaled_x.reshape(block_count, SPAN, MH, MP), log_decay.reshape(block_count, SPAN, MH), in_basis.reshape(block_count, SPAN, NS), out_basis.reshape(block_count, SPAN, NS))
    start_state = jnp.zeros((MH, MP, NS), jnp.float32)
    end_state, results = lax.scan(jax.checkpoint(span_step), start_state, pieces)
    mixed = results.reshape(count_of_rows, MH, MP) + skip_weight[None, :, None] * per_head
    return mixed.reshape(count_of_rows, MH * MP) * sigmoid_linear(gate_raw)

def attention(query_rows, key_rows, value_rows):
    count_of_rows = query_rows.shape[0]
    head_groups = QUERY_HEADS // KEY_VALUE_HEADS
    scale = HEAD_SIZE ** (-0.5)
    rows_per_block = min(512, count_of_rows)
    heads_for_queries = query_rows.reshape(count_of_rows, KEY_VALUE_HEADS, head_groups, HEAD_SIZE)
    heads_for_keys = key_rows.reshape(count_of_rows, KEY_VALUE_HEADS, HEAD_SIZE)
    heads_for_values = value_rows.reshape(count_of_rows, KEY_VALUE_HEADS, HEAD_SIZE)
    key_place = jnp.arange(count_of_rows)

    def one_block(start_row):
        block_of_queries = lax.dynamic_slice_in_dim(heads_for_queries, start_row, rows_per_block, 0)
        scores = jnp.einsum('qkgd,tkd->kgqt', block_of_queries, heads_for_keys, precision=highest) * scale
        scores = low_back(scores)
        query_place = start_row + jnp.arange(rows_per_block)
        scores = jnp.where(key_place[None, :] <= query_place[:, None], scores, masked_score)
        weights = jnp.exp(scores - lax.optimization_barrier(jnp.max(scores, axis=-1, keepdims=True)))
        probs = low(weights / lax.optimization_barrier(jnp.sum(weights, axis=-1, keepdims=True)))
        mixed = jnp.einsum('kgqt,tkd->qkgd', probs, heads_for_values, precision=highest)
        return mixed.reshape(rows_per_block, QUERY_HEADS * HEAD_SIZE)
    starts = jnp.arange(count_of_rows // rows_per_block).astype(jnp.int32) * rows_per_block
    return lax.map(jax.checkpoint(one_block), starts).reshape(count_of_rows, QUERY_HEADS * HEAD_SIZE)

def layer_forward(hidden, weights):
    mixer_w, attn_w, mamba_w, attn_out_w, gate_up_w, down_w, scales, step_shift, decay_rate, skip_weight = weights
    inner = MH * MP
    query_width = QUERY_HEADS * HEAD_SIZE
    width_of_keys = KEY_VALUE_HEADS * HEAD_SIZE
    normed = low(norm_rows(hidden, scales[0]))
    projected = low_back(matmul_high(normed, mixer_w))
    attn_rows = low(low_back(matmul_high(normed, attn_w)))
    gated = mamba_mix(projected[:, :inner], projected[:, inner:2 * inner], projected[:, 2 * inner:2 * inner + NS], projected[:, 2 * inner + NS:2 * inner + 2 * NS], projected[:, 2 * inner + 2 * NS:], step_shift, decay_rate, skip_weight)
    gated = low(low_back(gated))
    mamba_branch = low_back(matmul_high(gated, mamba_w))
    attn_mixed = attention(attn_rows[:, :query_width], attn_rows[:, query_width:query_width + width_of_keys], attn_rows[:, query_width + width_of_keys:])
    attn_mixed = low(low_back(attn_mixed))
    attn_branch = low_back(matmul_high(attn_mixed, attn_out_w))
    after_mixers = hidden + attn_branch + mamba_branch
    normed_two = low(norm_rows(after_mixers, scales[1]))
    gate_rows = low_back(matmul_high(normed_two, gate_up_w))
    activated = low(low_back(sigmoid_linear(gate_rows[:, :FF]) * gate_rows[:, FF:]))
    return after_mixers + low_back(matmul_high(activated, down_w))

def reference(inputs, cotangent, mixer_in, attn_in, mamba_out, attn_out, gate_up, down_proj, norm_gains, step_bias, decay_log, skip_gain):
    params = tuple((item.astype(jnp.float32) for item in (mixer_in, attn_in, mamba_out, attn_out, gate_up, down_proj, norm_gains, step_bias, decay_log, skip_gain)))

    def forward(sequence, weights_all):
        hidden = sequence
        for layer_index in range(LAYERS):
            hidden = layer_forward(hidden, tuple((item[layer_index] for item in weights_all)))
        return hidden

    def per_sequence(totals, pair):
        sequence, grad_in = pair
        result, back_fn = jax.vjp(forward, sequence.astype(jnp.float32), params)
        input_part, param_grads = back_fn(grad_in.astype(jnp.float32))
        totals = tuple((left + right for left, right in zip(totals, param_grads)))
        return (totals, (result.astype(jnp.bfloat16), input_part))
    zeros_start = tuple((jnp.zeros(item.shape, jnp.float32) for item in params))
    totals, (results, input_parts) = lax.scan(per_sequence, zeros_start, (inputs, cotangent))
    return (results, input_parts, totals[0], totals[1], totals[2], totals[3], totals[4], totals[5], totals[6], totals[7], totals[8], totals[9])
```

```python
import jax
import jax.numpy as jnp
from jax import lax
from jax.experimental import pallas as pl
from jax.experimental.pallas import tpu as pltpu
from jax.sharding import PartitionSpec as P

MH = 24
MP = 64
NS = 128
QH = 8
KVH = 2
HS = 64
FF = 2048
SEQ = 8
DP = 16
HL = MH // SEQ
HW = HL * MP
INNER = MH * MP
FL = FF // SEQ
ROWS = 128
TOK = 1024
D = 1024
CH = 256
NCH = TOK // CH
CB, CC, CZ, CQ, CU, CK, CV, CR, CW = 0, 128, 256, 448, 512, 704, 768, 832, 896
EPS = 1e-05
NEG = -1e30
F32 = jnp.float32
BF = jnp.bfloat16
HIGH = lax.Precision.HIGHEST


def dot(a, b, dims=((1,), (0,)), precision=None):
    return lax.dot_general(a, b, (dims, ((), ())), precision=precision, preferred_element_type=F32)


def x_shift(k):
    return [(i, ((i // 2 + k) % 4) * 2 + i % 2) for i in range(SEQ)]


Z_SWAP = [(i, i ^ 1) for i in range(SEQ)]


def gather_rows(x):
    me = lax.axis_index("seq")
    mx, mz = me // 2, me % 2
    h = x.shape[0] // 2
    send = lambda v, perm: lax.ppermute(v, "seq", perm)
    z, a, b = send(x, Z_SWAP), send(x, x_shift(1)), send(x, x_shift(-1))
    c0, c1 = send(a[:h], x_shift(1)), send(b[h:], x_shift(-1))
    za, zb = send(z, x_shift(1)), send(z, x_shift(-1))
    zc0, zc1 = send(c0, Z_SWAP), send(c1, Z_SWAP)
    out = jnp.zeros((TOK, x.shape[1]), x.dtype)

    def put(out, v, dx, other, off):
        at = ((mx + dx) % 4 * 2 + (1 - mz if other else mz)) * ROWS + off
        return lax.dynamic_update_slice(out, v, (at, 0))

    for v, dx, other, off in (
        (x, 0, 0, 0), (z, 0, 1, 0), (a, 3, 0, 0), (b, 1, 0, 0), (c0, 2, 0, 0), (c1, 2, 0, h),
        (za, 3, 1, 0), (zb, 1, 1, 0), (zc0, 2, 1, 0), (zc1, 2, 1, h),
    ):
        out = put(out, v, dx, other, off)
    return out


def scatter_rows(part):
    got = lax.all_to_all(part.reshape(SEQ, ROWS, D), "seq", split_axis=0, concat_axis=0, tiled=True)
    return got.astype(F32).sum(0)


def per_head(cols, shape):
    lane = lax.broadcasted_iota(jnp.int32, shape, 1)
    return jnp.where(lane < MP, cols[0], jnp.where(lane < 2 * MP, cols[1], cols[2]))


def widen(v8):
    return per_head([v8[:, h : h + 1] for h in range(HL)], (v8.shape[0], HW))


def row_heads(v8):
    row = lax.broadcasted_iota(jnp.int32, (HW, NS), 0)
    return jnp.where(row < MP, v8[:, 0:1], jnp.where(row < 2 * MP, v8[:, 1:2], v8[:, 2:3]))


def head_mask(h, shape):
    lane = lax.broadcasted_iota(jnp.int32, shape, 1)
    return (lane >= h * MP) & (lane < (h + 1) * MP)


def tri_lower():
    t = lax.broadcasted_iota(jnp.int32, (CH, CH), 0)
    s = lax.broadcasted_iota(jnp.int32, (CH, CH), 1)
    return t >= s


def steps(r8, small):
    pre = r8 + small[0:1, :]
    dt = jnp.log1p(jnp.exp(pre))
    return pre, dt, -jnp.exp(small[1:2, :]) * dt


def block_decays(log_decay):
    low = tri_lower()
    ones = low.astype(F32)
    cum = dot(ones, log_decay, precision=HIGH)
    cum_t = dot(log_decay, ones, ((0,), (1,)), precision=HIGH)
    decays = [
        jnp.exp(jnp.where(low, cum[:, h : h + 1] - cum_t[h : h + 1, :], NEG)) for h in range(HL)
    ]
    return cum, decays


def causal(c, scores):
    t = c * CH + lax.broadcasted_iota(jnp.int32, scores.shape, 0)
    s = lax.broadcasted_iota(jnp.int32, scores.shape, 1)
    return jnp.where(s <= t, scores, NEG)


def mixer_forward_kernel(proj, small_ref, mix, y_out, states, log_totals, keys, values):
    small = small_ref[...]
    state = jnp.zeros((HW, NS), F32)
    for c in range(NCH):
        rows = slice(c * CH, (c + 1) * CH)
        b = proj[rows, CB : CB + NS].astype(BF)
        cc = proj[rows, CC : CC + NS].astype(BF)
        z = proj[rows, CZ : CZ + HW]
        u = proj[rows, CU : CU + HW]
        _, dt, log_decay = steps(proj[rows, CR : CR + 8], small)
        cum, decays = block_decays(log_decay)
        g = dot(cc, b, ((1,), (1,)))
        v = u * widen(dt)
        vb = v.astype(BF)
        intra = [dot((m * g).astype(BF), vb) for m in decays]
        last = cum[CH - 1 : CH, :]
        y = per_head(intra, (CH, HW)) + widen(jnp.exp(cum)) * dot(
            cc, state.astype(BF), ((1,), (1,))
        )
        states[c] = state
        state = row_heads(jnp.exp(last)) * state + dot(
            (v * widen(jnp.exp(last - cum))).astype(BF), b, ((0,), (0,))
        )
        y = y + widen(jnp.broadcast_to(small[2:3, :], (CH, 8))) * u
        y_out[rows, :] = y
        mix[rows, 0:HW] = (y * z * jax.nn.sigmoid(z)).astype(BF)

        q = proj[rows, CQ : CQ + HS].astype(BF)
        keys[rows, :] = proj[rows, CK : CK + HS].astype(BF)
        values[rows, :] = proj[rows, CV : CV + HS].astype(BF)
        seen = (c + 1) * CH
        scores = causal(c, dot(q, keys[0:seen, :], ((1,), (1,))) * HS**-0.5)
        peak = jnp.max(scores, axis=1, keepdims=True)
        weights = jnp.exp(scores - peak)
        totals = jnp.sum(weights, axis=1, keepdims=True)
        probs = (weights / totals).astype(BF)
        mix[rows, HW : HW + HS] = dot(probs, values[0:seen, :]).astype(BF)
        log_totals[rows, :] = jnp.broadcast_to(peak + jnp.log(totals), (CH, 8))


def mixer_backward_kernel(
    proj, small_ref, y_in, states, log_totals, mix_grad, out, sums, keys, values, key_grad, value_grad
):
    small = small_ref[...]
    skip_w = widen(jnp.broadcast_to(small[2:3, :], (CH, 8)))
    keys[...] = proj[:, CK : CK + HS].astype(BF)
    values[...] = proj[:, CV : CV + HS].astype(BF)
    key_grad[...] = jnp.zeros_like(key_grad)
    value_grad[...] = jnp.zeros_like(value_grad)
    state_grad = jnp.zeros((HW, NS), F32)
    low = tri_lower()
    ones_low = low.astype(F32)
    lane8 = lax.broadcasted_iota(jnp.int32, (HW, 8), 1)
    row8 = lax.broadcasted_iota(jnp.int32, (HW, 8), 0)
    heads = (row8 // MP == lane8).astype(F32)
    lane_ch = lax.broadcasted_iota(jnp.int32, (CH, 8), 1)
    acc_bias = jnp.zeros((1, 8), F32)
    acc_decay = jnp.zeros((1, 8), F32)
    acc_skip = jnp.zeros((1, 8), F32)
    rate = jnp.exp(small[1:2, :])
    for c in reversed(range(NCH)):
        rows = slice(c * CH, (c + 1) * CH)
        seen = (c + 1) * CH
        q = proj[rows, CQ : CQ + HS].astype(BF)
        grad = mix_grad[rows, HW : HW + HS].astype(BF)
        scores = causal(c, dot(q, keys[0:seen, :], ((1,), (1,))) * HS**-0.5)
        probs = jnp.exp(scores - log_totals[rows, 0:1])
        prob_grad = dot(grad, values[0:seen, :], ((1,), (1,)))
        weighted = probs * prob_grad
        centre = jnp.sum(weighted, axis=1, keepdims=True)
        score_grad = (weighted - probs * centre).astype(BF)
        query_grad = dot(score_grad, keys[0:seen, :]) * HS**-0.5
        key_grad[0:seen, :] += dot(score_grad, q, ((0,), (0,)))
        value_grad[0:seen, :] += dot(probs.astype(BF), grad, ((0,), (0,)))
        out[rows, CQ : CQ + HS] = query_grad.astype(BF)
        out[rows, CK : CK + HS] = (key_grad[rows, :] * HS**-0.5).astype(BF)
        out[rows, CV : CV + HS] = value_grad[rows, :].astype(BF)

        b = proj[rows, CB : CB + NS].astype(BF)
        cc = proj[rows, CC : CC + NS].astype(BF)
        z = proj[rows, CZ : CZ + HW]
        u = proj[rows, CU : CU + HW]
        pre, dt, log_decay = steps(proj[rows, CR : CR + 8], small)
        cum, decays = block_decays(log_decay)
        last = cum[CH - 1 : CH, :]
        g = dot(cc, b, ((1,), (1,)))
        dt_w = widen(dt)
        v = u * dt_w
        vb = v.astype(BF)
        gated_grad = mix_grad[rows, 0:HW].astype(BF).astype(F32)
        gate = jax.nn.sigmoid(z)
        dy = gated_grad * z * gate
        out[rows, CZ : CZ + HW] = (
            gated_grad * y_in[rows, :] * gate * (1.0 + z * (1.0 - gate))
        ).astype(BF)
        dyb = dy.astype(BF)
        state = states[c]
        sb = state.astype(BF)
        qb = state_grad.astype(BF)
        grow = widen(jnp.exp(cum))
        fade = widen(jnp.exp(last - cum))
        v_grad_inter = fade * dot(b, qb, ((1,), (1,)))
        y_inter = grow * dot(cc, sb, ((1,), (1,)))
        g_grad = jnp.zeros((CH, CH), F32)
        v_grads = []
        cum_grad = jnp.zeros((CH, 8), F32)
        for h in range(HL):
            pair = dot(jnp.where(head_mask(h, (CH, HW)), dyb, jnp.zeros_like(dyb)), vb, ((1,), (1,)))
            mixed_pair = decays[h] * pair
            g_grad = g_grad + mixed_pair
            v_grads.append(dot((decays[h] * g).astype(BF), dyb, ((0,), (0,))))
            swing = (mixed_pair * g).astype(BF)
            one = (lane_ch == h).astype(BF)
            cum_grad = cum_grad + dot(swing, one) - dot(swing, one, ((0,), (0,)))
        v_grad = per_head(v_grads, (CH, HW)) + v_grad_inter
        g_gradb = g_grad.astype(BF)
        grown = (grow * dy).astype(BF)
        out[rows, CC : CC + NS] = (dot(g_gradb, b) + dot(grown, sb)).astype(BF)
        out[rows, CB : CB + NS] = (
            dot(g_gradb, cc, ((0,), (0,))) + dot((fade * v).astype(BF), qb)
        ).astype(BF)
        out[rows, CU : CU + HW] = (skip_w * dy + dt_w * v_grad).astype(BF)
        per_state = dot(heads, state * state_grad, ((0,), (0,)), precision=HIGH)
        over = dot(jnp.ones((8, NS), F32), per_state, ((1,), (1,)), precision=HIGH)[0:1, :]
        behind = dot(v * v_grad_inter, heads, precision=HIGH)
        ahead = cum_grad + dot(dy * y_inter, heads, precision=HIGH)
        decay_grad = (
            dot(ones_low, ahead, ((0,), (0,)), precision=HIGH)
            + dot(ones_low, behind, precision=HIGH)
            - behind
            + jnp.exp(last) * over
        )
        step_grad = dot(u * v_grad, heads, precision=HIGH) - rate * decay_grad
        r_grad = step_grad * jax.nn.sigmoid(pre)
        out[rows, CR : CR + HS] = jnp.concatenate(
            [r_grad, jnp.zeros((CH, HS - 8), F32)], axis=1
        ).astype(BF)
        acc_bias = acc_bias + jnp.sum(r_grad, axis=0, keepdims=True)
        acc_decay = acc_decay - rate * jnp.sum(dt * decay_grad, axis=0, keepdims=True)
        acc_skip = acc_skip + dot(
            jnp.broadcast_to(jnp.sum(dy * u, axis=0, keepdims=True), (8, HW)), heads, precision=HIGH
        )[0:1, :]
        state_grad = row_heads(jnp.exp(last)) * state_grad + dot(grown, cc, ((0,), (0,)))
    sums[...] = jnp.concatenate([acc_bias, acc_decay, acc_skip, jnp.zeros((5, 8), F32)], axis=0)


VMEM = pl.BlockSpec(memory_space=pltpu.VMEM)
PARAMS = pltpu.CompilerParams(vmem_limit_bytes=50 * 1024 * 1024)


def mixer_forward(proj, small):
    return pl.pallas_call(
        mixer_forward_kernel,
        out_shape=(
            jax.ShapeDtypeStruct((TOK, HW + HS), BF),
            jax.ShapeDtypeStruct((TOK, HW), F32),
            jax.ShapeDtypeStruct((NCH, HW, NS), F32),
            jax.ShapeDtypeStruct((TOK, 8), F32),
        ),
        in_specs=[VMEM] * 2,
        out_specs=(VMEM,) * 4,
        scratch_shapes=[pltpu.VMEM((TOK, HS), BF), pltpu.VMEM((TOK, HS), BF)],
        compiler_params=PARAMS,
    )(proj, small)


def mixer_backward(proj, small, y, states, log_totals, mix_grad):
    return pl.pallas_call(
        mixer_backward_kernel,
        out_shape=(jax.ShapeDtypeStruct((TOK, CW), BF), jax.ShapeDtypeStruct((8, 8), F32)),
        in_specs=[VMEM] * 6,
        out_specs=(VMEM,) * 2,
        scratch_shapes=[
            pltpu.VMEM((TOK, HS), BF),
            pltpu.VMEM((TOK, HS), BF),
            pltpu.VMEM((TOK, HS), F32),
            pltpu.VMEM((TOK, HS), F32),
        ],
        compiler_params=PARAMS,
    )(proj, small, y, states, log_totals, mix_grad)


def mixer_shares(mixer_w, attn_w):
    z = mixer_w[:, :INNER].reshape(ROWS, SEQ, HW).swapaxes(0, 1)
    u = mixer_w[:, INNER : 2 * INNER].reshape(ROWS, SEQ, HW).swapaxes(0, 1)
    both = jnp.broadcast_to(mixer_w[None, :, 2 * INNER : 2 * INNER + 2 * NS], (SEQ, ROWS, 2 * NS))
    r = mixer_w[:, 2 * INNER + 2 * NS :].reshape(ROWS, SEQ, HL).swapaxes(0, 1)
    q = attn_w[:, : QH * HS].reshape(ROWS, SEQ, HS).swapaxes(0, 1)

    def kv(w):
        w = w.reshape(ROWS, KVH, HS).swapaxes(0, 1)
        return jnp.repeat(w, SEQ // KVH, axis=0)

    k = kv(attn_w[:, QH * HS : QH * HS + KVH * HS])
    v = kv(attn_w[:, QH * HS + KVH * HS :])
    pad = jnp.zeros((SEQ, ROWS, CW - CR - HL), mixer_w.dtype)
    return jnp.concatenate([both, z, q, u, k, v, r, pad], axis=2)


def mixer_rows(shares):
    n = shares.shape[1]
    flat = lambda v: v.swapaxes(0, 1).reshape(n, -1)

    def kv(v):
        return flat(v.reshape(KVH, SEQ // KVH, n, HS).sum(1))

    both = shares[:, :, : 2 * NS].sum(0)
    mixer = [
        flat(shares[:, :, CZ : CZ + HW]),
        flat(shares[:, :, CU : CU + HW]),
        both,
        flat(shares[:, :, CR : CR + HL]),
    ]
    attn = [
        flat(shares[:, :, CQ : CQ + HS]),
        kv(shares[:, :, CK : CK + HS]),
        kv(shares[:, :, CV : CV + HS]),
    ]
    sums = shares[:, :, CR + 8 : CR + 8 + 3 * HL].sum(0)
    return jnp.concatenate(mixer + attn + [sums], axis=1)


def unit_rows(x):
    return x * lax.rsqrt(jnp.mean(x * x, axis=-1, keepdims=True) + EPS)


def unit_back(x, e):
    rho = lax.rsqrt(jnp.mean(x * x, axis=-1, keepdims=True) + EPS)
    return rho * e - x * (rho * rho * rho) * jnp.mean(x * e, axis=-1, keepdims=True)


def local(
    inputs, cotangent, mixer_in, attn_in, mamba_out, attn_out, gate_up, down_proj,
    norm_gains, step_bias, decay_log, skip_gain,
):
    me = lax.axis_index("seq")
    x0 = inputs[0]
    gains = norm_gains[0].astype(F32)
    g1, g2 = gains[0][:, None], gains[1][:, None]
    mixer_f = mixer_in[0].astype(F32)
    attn_f = attn_in[0].astype(F32)
    gate_up_f = gate_up[0].astype(F32)
    down_w = down_proj[0]
    out_w = jnp.concatenate([mamba_out[0], attn_out[0]], axis=0)
    small = jnp.zeros((8, 8), F32)
    small = small.at[0, :HL].set(step_bias[0].astype(F32))
    small = small.at[1, :HL].set(decay_log[0].astype(F32))
    small = small.at[2, :HL].set(skip_gain[0].astype(F32))

    shares = mixer_shares((mixer_f * g1).astype(BF), (attn_f * g1).astype(BF))
    in_w = lax.all_to_all(shares, "seq", split_axis=0, concat_axis=0, tiled=True).reshape(D, CW)
    x_all = gather_rows(x0)
    unit_one = unit_rows(x_all.astype(F32)).astype(BF)
    proj = dot(unit_one, in_w)
    mix, y, states, log_totals = mixer_forward(proj, small)
    mid = scatter_rows(dot(mix, out_w).astype(BF)) + x0.astype(F32)

    gu = (gate_up_f * g2).astype(BF).reshape(ROWS, 2, SEQ, FL).transpose(2, 0, 1, 3)
    gu_w = lax.all_to_all(gu, "seq", split_axis=0, concat_axis=0, tiled=True).reshape(D, 2 * FL)
    ffn_grad = lax.all_gather(cotangent[0], "seq", axis=0, tiled=True)
    unit_two = gather_rows(unit_rows(mid).astype(BF))
    gate_rows = dot(unit_two, gu_w)
    gate, wide = gate_rows[:, :FL], gate_rows[:, FL:]
    s = jax.nn.sigmoid(gate)
    act = (gate * s * wide).astype(BF)
    act_grad = dot(ffn_grad, down_w, ((1,), (1,))).astype(BF).astype(F32)
    up_grad = jnp.concatenate(
        [act_grad * wide * s * (1.0 + gate * (1.0 - s)), act_grad * gate * s], axis=1
    ).astype(BF)
    mid_e = scatter_rows(dot(up_grad, gu_w, ((1,), (1,))).astype(BF))
    mid_grad = cotangent[0].astype(F32) + unit_back(mid, mid_e)
    branch = gather_rows(mid_grad.astype(BF))

    result = lax.psum_scatter(
        dot(act, down_w).astype(BF), "seq", scatter_dimension=0, tiled=True
    ).astype(F32)
    outputs = (mid + result).astype(BF)
    down_grad = dot(act, ffn_grad, ((0,), (0,))).astype(BF)
    gu_grad = dot(unit_two, up_grad, ((0,), (0,))).astype(BF)
    gu_grad = lax.all_to_all(
        gu_grad.reshape(SEQ, ROWS, 2 * FL), "seq", split_axis=0, concat_axis=0, tiled=True
    )
    gu_grad = gu_grad.reshape(SEQ, ROWS, 2, FL).transpose(1, 2, 0, 3).reshape(ROWS * 4, D)
    ffn_sums = lax.psum(jnp.concatenate([gu_grad, down_grad], axis=0), "dp").astype(F32)
    gate_up_grad = ffn_sums[: ROWS * 4].reshape(ROWS, 2 * FF)
    down_sum = ffn_sums[ROWS * 4 :]

    mix_grad = dot(branch, out_w, ((1,), (1,)))
    out_grad = lax.psum(dot(mix, branch, ((0,), (0,))).astype(BF), "dp").astype(F32)
    proj_grad, sums = mixer_backward(proj, small, y, states, log_totals, mix_grad)
    in_grad = dot(unit_one, proj_grad, ((0,), (0,)))
    line = jnp.concatenate([sums[0, :HL], sums[1, :HL], sums[2, :HL]])[None]
    in_grad = lax.dynamic_update_slice(in_grad, line, (me * ROWS, CR + 8)).astype(BF)
    sent = in_grad.reshape(SEQ, DP, ROWS // DP, CW).swapaxes(0, 1).reshape(DP * SEQ, ROWS // DP, CW)
    got = lax.all_to_all(sent, ("dp", "seq"), split_axis=0, concat_axis=0, tiled=True)
    got = got.reshape(DP, SEQ, ROWS // DP, CW).astype(F32).sum(0)
    rows = mixer_rows(got).astype(BF)
    in_e = scatter_rows(dot(proj_grad, in_w, ((1,), (1,))).astype(BF))
    input_grad = mid_grad + unit_back(x0.astype(F32), in_e)
    rows = lax.all_gather(rows, "dp", axis=0, tiled=True).astype(F32)
    wm = 2 * INNER + 2 * NS + MH
    wa = (QH + 2 * KVH) * HS
    mixer_rows_grad = rows[:, :wm]
    attn_rows_grad = rows[:, wm : wm + wa]
    line = rows[0, wm + wa :]
    gain_one = (mixer_rows_grad * mixer_f).sum(1) + (attn_rows_grad * attn_f).sum(1)
    gain_two = (gate_up_grad * gate_up_f).sum(1)
    return (
        outputs[None],
        input_grad[None],
        (mixer_rows_grad * g1)[None],
        (attn_rows_grad * g1)[None],
        out_grad[None, :HW],
        out_grad[None, HW:],
        (gate_up_grad * g2)[None],
        down_sum[None],
        jnp.stack([gain_one, gain_two])[None],
        line[None, :HL],
        line[None, HL : 2 * HL],
        line[None, 2 * HL : 3 * HL],
    )


def solution(mesh):
    rows = P("dp", "seq", None)
    owned = P(None, "seq", None)
    heads = P(None, "seq")
    gains = P(None, None, "seq")
    return jax.shard_map(
        local,
        mesh=mesh,
        in_specs=(rows, rows) + (owned,) * 6 + (gains,) + (heads,) * 3,
        out_specs=(rows, rows) + (owned,) * 6 + (gains,) + (heads,) * 3,
        check_vma=False,
    )
```

```python
import jax
import jax.numpy as jnp
from jax import lax
from jax.experimental import pallas as pl
from jax.experimental.pallas import tpu as pltpu
from jax.sharding import PartitionSpec as P

MH = 24
MP = 64
NS = 128
QH = 8
KVH = 2
HS = 64
FF = 2048
SEQ = 8
DP = 16
HL = MH // SEQ
HW = HL * MP
INNER = MH * MP
FL = FF // SEQ
ROWS = 128
TOK = 1024
D = 1024
CH = 256
NCH = TOK // CH
CB, CC, CZ, CQ, CU, CK, CV, CR, CW = 0, 128, 256, 448, 512, 704, 768, 832, 896
EPS = 1e-05
NEG = -1e30
F32 = jnp.float32
BF = jnp.bfloat16
HIGH = lax.Precision.HIGHEST


def dot(a, b, dims=((1,), (0,)), precision=None):
    return lax.dot_general(a, b, (dims, ((), ())), precision=precision, preferred_element_type=F32)


def x_shift(k):
    return [(i, ((i // 2 + k) % 4) * 2 + i % 2) for i in range(SEQ)]


Z_SWAP = [(i, i ^ 1) for i in range(SEQ)]


PLACES = (
    (0, 0, 0), (0, 1, 0), (3, 0, 0), (1, 0, 0), (2, 0, 0), (2, 0, 64), (3, 1, 0), (1, 1, 0), (2, 1, 0), (2, 1, 64),
)


def gather_pieces(x):
    h = x.shape[0] // 2
    send = lambda v, perm: lax.ppermute(v, "seq", perm)
    z, a, b = send(x, Z_SWAP), send(x, x_shift(1)), send(x, x_shift(-1))
    c0, c1 = send(a[:h], x_shift(1)), send(b[h:], x_shift(-1))
    za, zb = send(z, x_shift(1)), send(z, x_shift(-1))
    zc0, zc1 = send(c0, Z_SWAP), send(c1, Z_SWAP)
    return x, z, a, b, c0, c1, za, zb, zc0, zc1


def piece_row(me, place):
    dx, other, off = place
    mx, mz = me // 2, me % 2
    mz = 1 - mz if other else mz
    return pl.multiple_of(((mx + dx) % 4 * 2 + mz) * ROWS + off, 64)


def scatter_rows(part, beside=()):
    got = lax.all_to_all(part.reshape(SEQ, ROWS, D), "seq", split_axis=0, concat_axis=0, tiled=True)
    if not beside:
        return got.astype(F32).sum(0)
    got, *beside = lax.optimization_barrier((got, *beside))
    return got.astype(F32).sum(0), beside


def scatter_rows_direct(part, me):
    part = part.reshape(SEQ, ROWS, D)
    total = lax.dynamic_index_in_dim(part, me, 0, False).astype(F32)
    got = []
    for k in range(1, SEQ):
        own = lax.dynamic_index_in_dim(part, me ^ k, 0, False)
        got.append(lax.ppermute(own, "seq", [(i, i ^ k) for i in range(SEQ)]))
    for v in got:
        total = total + v.astype(F32)
    return total


def core_swap(v):
    return lax.ppermute(v, "dp", [(i, i ^ 1) for i in range(DP)])


def same_core():
    return [[d * SEQ + s for d in range(c, DP, 2) for s in range(SEQ)] for c in range(2)]


def per_head(cols, shape):
    lane = lax.broadcasted_iota(jnp.int32, shape, 1)
    return jnp.where(lane < MP, cols[0], jnp.where(lane < 2 * MP, cols[1], cols[2]))


def widen(v8):
    return per_head([v8[:, h : h + 1] for h in range(HL)], (v8.shape[0], HW))


def row_heads(v8):
    row = lax.broadcasted_iota(jnp.int32, (HW, NS), 0)
    return jnp.where(row < MP, v8[:, 0:1], jnp.where(row < 2 * MP, v8[:, 1:2], v8[:, 2:3]))


def head_mask(h, shape):
    lane = lax.broadcasted_iota(jnp.int32, shape, 1)
    return (lane >= h * MP) & (lane < (h + 1) * MP)


def tri_lower():
    t = lax.broadcasted_iota(jnp.int32, (CH, CH), 0)
    s = lax.broadcasted_iota(jnp.int32, (CH, CH), 1)
    return t >= s


def steps(r8, small):
    pre = r8 + small[0:1, :]
    dt = jnp.log1p(jnp.exp(pre))
    return pre, dt, -jnp.exp(small[1:2, :]) * dt


def block_decays(log_decay):
    low = tri_lower()
    ones = low.astype(F32)
    cum = dot(ones, log_decay, precision=HIGH)
    cum_t = dot(log_decay, ones, ((0,), (1,)), precision=HIGH)
    decays = [
        jnp.exp(jnp.where(low, cum[:, h : h + 1] - cum_t[h : h + 1, :], NEG)) for h in range(HL)
    ]
    return cum, decays


def causal(c, scores):
    t = c * CH + lax.broadcasted_iota(jnp.int32, scores.shape, 0)
    s = lax.broadcasted_iota(jnp.int32, scores.shape, 1)
    return jnp.where(s <= t, scores, NEG)


def unit_rows(x):
    return x * lax.rsqrt(jnp.mean(x * x, axis=-1, keepdims=True) + EPS)


def mixer_forward_kernel(*refs):
    (
        where, w_mine, w_other, small_ref, out_w, *pieces,
        unit, ffn_grad, in_w, gu_w, proj, mix, y_out, states, log_totals, mid_part, keys, values,
    ) = refs
    me, core = where[0], where[1]
    for piece, place in zip(pieces, PLACES):
        rows = pl.ds(piece_row(me, place), piece.shape[0])
        unit[rows, :] = unit_rows(piece[:, :D].astype(F32)).astype(BF)
        ffn_grad[rows, :] = piece[:, D:]
    half = ROWS // 2
    for j in range(SEQ):
        for source, at in ((w_mine, core * half), (w_other, half - core * half)):
            rows = pl.ds(pl.multiple_of(at + j * ROWS, half), half)
            in_w[rows, :] = source[j, :, :CW]
            gu_w[rows, :] = source[j, :, CW:]
    small = small_ref[...]
    state = jnp.zeros((HW, NS), F32)
    for c in range(NCH):
        rows = slice(c * CH, (c + 1) * CH)
        proj[rows, :] = dot(unit[rows, :], in_w[...])
        b = proj[rows, CB : CB + NS].astype(BF)
        cc = proj[rows, CC : CC + NS].astype(BF)
        z = proj[rows, CZ : CZ + HW]
        u = proj[rows, CU : CU + HW]
        _, dt, log_decay = steps(proj[rows, CR : CR + 8], small)
        cum, decays = block_decays(log_decay)
        g = dot(cc, b, ((1,), (1,)))
        v = u * widen(dt)
        vb = v.astype(BF)
        intra = [dot((m * g).astype(BF), vb) for m in decays]
        last = cum[CH - 1 : CH, :]
        y = per_head(intra, (CH, HW)) + widen(jnp.exp(cum)) * dot(
            cc, state.astype(BF), ((1,), (1,))
        )
        states[c] = state
        state = row_heads(jnp.exp(last)) * state + dot(
            (v * widen(jnp.exp(last - cum))).astype(BF), b, ((0,), (0,))
        )
        y = y + widen(jnp.broadcast_to(small[2:3, :], (CH, 8))) * u
        y_out[rows, :] = y
        mix[rows, 0:HW] = (y * z * jax.nn.sigmoid(z)).astype(BF)

        q = proj[rows, CQ : CQ + HS].astype(BF)
        keys[rows, :] = proj[rows, CK : CK + HS].astype(BF)
        values[rows, :] = proj[rows, CV : CV + HS].astype(BF)
        seen = (c + 1) * CH
        scores = causal(c, dot(q, keys[0:seen, :], ((1,), (1,))) * HS**-0.5)
        peak = jnp.max(scores, axis=1, keepdims=True)
        weights = jnp.exp(scores - peak)
        totals = jnp.sum(weights, axis=1, keepdims=True)
        probs = (weights / totals).astype(BF)
        mix[rows, HW : HW + HS] = dot(probs, values[0:seen, :]).astype(BF)
        log_totals[rows, :] = jnp.broadcast_to(peak + jnp.log(totals), (CH, 8))
        mid_part[rows, :] = dot(mix[rows, :], out_w[...]).astype(BF)


def mixer_backward_kernel(
    proj, small_ref, y_in, states, log_totals, mix_grad, out, sums, keys, values, key_grad, value_grad
):
    small = small_ref[...]
    skip_w = widen(jnp.broadcast_to(small[2:3, :], (CH, 8)))
    keys[...] = proj[:, CK : CK + HS].astype(BF)
    values[...] = proj[:, CV : CV + HS].astype(BF)
    key_grad[...] = jnp.zeros_like(key_grad)
    value_grad[...] = jnp.zeros_like(value_grad)
    state_grad = jnp.zeros((HW, NS), F32)
    low = tri_lower()
    ones_low = low.astype(F32)
    lane8 = lax.broadcasted_iota(jnp.int32, (HW, 8), 1)
    row8 = lax.broadcasted_iota(jnp.int32, (HW, 8), 0)
    heads = (row8 // MP == lane8).astype(F32)
    lane_ch = lax.broadcasted_iota(jnp.int32, (CH, 8), 1)
    acc_bias = jnp.zeros((1, 8), F32)
    acc_decay = jnp.zeros((1, 8), F32)
    acc_skip = jnp.zeros((1, 8), F32)
    rate = jnp.exp(small[1:2, :])
    for c in reversed(range(NCH)):
        rows = slice(c * CH, (c + 1) * CH)
        seen = (c + 1) * CH
        q = proj[rows, CQ : CQ + HS].astype(BF)
        grad = mix_grad[rows, HW : HW + HS]
        scores = causal(c, dot(q, keys[0:seen, :], ((1,), (1,))) * HS**-0.5)
        probs = jnp.exp(scores - log_totals[rows, 0:1])
        prob_grad = dot(grad, values[0:seen, :], ((1,), (1,)))
        weighted = probs * prob_grad
        centre = jnp.sum(weighted, axis=1, keepdims=True)
        score_grad = (weighted - probs * centre).astype(BF)
        query_grad = dot(score_grad, keys[0:seen, :]) * HS**-0.5
        key_grad[0:seen, :] += dot(score_grad, q, ((0,), (0,)))
        value_grad[0:seen, :] += dot(probs.astype(BF), grad, ((0,), (0,)))
        out[rows, CQ : CQ + HS] = query_grad.astype(BF)
        out[rows, CK : CK + HS] = (key_grad[rows, :] * HS**-0.5).astype(BF)
        out[rows, CV : CV + HS] = value_grad[rows, :].astype(BF)

        b = proj[rows, CB : CB + NS].astype(BF)
        cc = proj[rows, CC : CC + NS].astype(BF)
        z = proj[rows, CZ : CZ + HW]
        u = proj[rows, CU : CU + HW]
        pre, dt, log_decay = steps(proj[rows, CR : CR + 8], small)
        cum, decays = block_decays(log_decay)
        last = cum[CH - 1 : CH, :]
        g = dot(cc, b, ((1,), (1,)))
        dt_w = widen(dt)
        v = u * dt_w
        vb = v.astype(BF)
        gated_grad = mix_grad[rows, 0:HW].astype(F32)
        gate = jax.nn.sigmoid(z)
        dy = gated_grad * z * gate
        out[rows, CZ : CZ + HW] = (
            gated_grad * y_in[rows, :] * gate * (1.0 + z * (1.0 - gate))
        ).astype(BF)
        dyb = dy.astype(BF)
        state = states[c]
        sb = state.astype(BF)
        qb = state_grad.astype(BF)
        grow = widen(jnp.exp(cum))
        fade = widen(jnp.exp(last - cum))
        v_grad_inter = fade * dot(b, qb, ((1,), (1,)))
        y_inter = grow * dot(cc, sb, ((1,), (1,)))
        g_grad = jnp.zeros((CH, CH), F32)
        v_grads = []
        cum_grad = jnp.zeros((CH, 8), F32)
        for h in range(HL):
            pair = dot(jnp.where(head_mask(h, (CH, HW)), dyb, jnp.zeros_like(dyb)), vb, ((1,), (1,)))
            mixed_pair = decays[h] * pair
            g_grad = g_grad + mixed_pair
            v_grads.append(dot((decays[h] * g).astype(BF), dyb, ((0,), (0,))))
            swing = (mixed_pair * g).astype(BF)
            one = (lane_ch == h).astype(BF)
            cum_grad = cum_grad + dot(swing, one) - dot(swing, one, ((0,), (0,)))
        v_grad = per_head(v_grads, (CH, HW)) + v_grad_inter
        g_gradb = g_grad.astype(BF)
        grown = (grow * dy).astype(BF)
        out[rows, CC : CC + NS] = (dot(g_gradb, b) + dot(grown, sb)).astype(BF)
        out[rows, CB : CB + NS] = (
            dot(g_gradb, cc, ((0,), (0,))) + dot((fade * v).astype(BF), qb)
        ).astype(BF)
        out[rows, CU : CU + HW] = (skip_w * dy + dt_w * v_grad).astype(BF)
        per_state = dot(heads, state * state_grad, ((0,), (0,)), precision=HIGH)
        over = dot(jnp.ones((8, NS), F32), per_state, ((1,), (1,)), precision=HIGH)[0:1, :]
        behind = dot(v * v_grad_inter, heads, precision=HIGH)
        ahead = cum_grad + dot(dy * y_inter, heads, precision=HIGH)
        decay_grad = (
            dot(ones_low, ahead, ((0,), (0,)), precision=HIGH)
            + dot(ones_low, behind, precision=HIGH)
            - behind
            + jnp.exp(last) * over
        )
        step_grad = dot(u * v_grad, heads, precision=HIGH) - rate * decay_grad
        r_grad = step_grad * jax.nn.sigmoid(pre)
        out[rows, CR : CR + HS] = jnp.concatenate(
            [r_grad, jnp.zeros((CH, HS - 8), F32)], axis=1
        ).astype(BF)
        acc_bias = acc_bias + jnp.sum(r_grad, axis=0, keepdims=True)
        acc_decay = acc_decay - rate * jnp.sum(dt * decay_grad, axis=0, keepdims=True)
        acc_skip = acc_skip + dot(
            jnp.broadcast_to(jnp.sum(dy * u, axis=0, keepdims=True), (8, HW)), heads, precision=HIGH
        )[0:1, :]
        state_grad = row_heads(jnp.exp(last)) * state_grad + dot(grown, cc, ((0,), (0,)))
    sums[...] = jnp.concatenate([acc_bias, acc_decay, acc_skip, jnp.zeros((5, 8), F32)], axis=0)


VMEM = pl.BlockSpec(memory_space=pltpu.VMEM)
PARAMS = pltpu.CompilerParams(vmem_limit_bytes=50 * 1024 * 1024)


SMEM = pl.BlockSpec(memory_space=pltpu.SMEM)


def mixer_forward(where, w_mine, w_other, small, out_w, pieces):
    shape = jax.ShapeDtypeStruct
    return pl.pallas_call(
        mixer_forward_kernel,
        out_shape=(
            shape((TOK, D), BF),
            shape((TOK, D), BF),
            shape((D, CW), BF),
            shape((D, 2 * FL), BF),
            shape((TOK, CW), F32),
            shape((TOK, HW + HS), BF),
            shape((TOK, HW), F32),
            shape((NCH, HW, NS), F32),
            shape((TOK, 8), F32),
            shape((TOK, D), BF),
        ),
        in_specs=[SMEM] + [VMEM] * 14,
        out_specs=(VMEM,) * 10,
        scratch_shapes=[pltpu.VMEM((TOK, HS), BF), pltpu.VMEM((TOK, HS), BF)],
        compiler_params=PARAMS,
    )(where, w_mine, w_other, small, out_w, *pieces)


def feed_forward_kernel(*refs):
    where, gu_w, act_grad, *pieces, unit, act, up_grad, e_part = refs
    for piece, place in zip(pieces, PLACES):
        unit[pl.ds(piece_row(where[0], place), piece.shape[0]), :] = piece[...]
    for c in range(NCH):
        rows = slice(c * CH, (c + 1) * CH)
        gate_rows = dot(unit[rows, :], gu_w[...])
        gate, wide = gate_rows[:, :FL], gate_rows[:, FL:]
        s = jax.nn.sigmoid(gate)
        act[rows, :] = (gate * s * wide).astype(BF)
        grad = act_grad[rows, :].astype(F32)
        up_grad[rows, :FL] = (grad * wide * s * (1.0 + gate * (1.0 - s))).astype(BF)
        up_grad[rows, FL:] = (grad * gate * s).astype(BF)
        e_part[rows, :] = dot(up_grad[rows, :], gu_w[...], ((1,), (1,))).astype(BF)


def feed_forward(where, gu_w, act_grad, pieces):
    shape = jax.ShapeDtypeStruct
    return pl.pallas_call(
        feed_forward_kernel,
        out_shape=(
            shape((TOK, D), BF), shape((TOK, FL), BF), shape((TOK, 2 * FL), BF), shape((TOK, D), BF),
        ),
        in_specs=[SMEM] + [VMEM] * 12,
        out_specs=(VMEM,) * 4,
        compiler_params=PARAMS,
    )(where, gu_w, act_grad, *pieces)


def branch_kernel(*refs):
    where, out_w, mix, *pieces, mix_grad, out_grad, branch = refs
    for piece, place in zip(pieces, PLACES):
        branch[pl.ds(piece_row(where[0], place), piece.shape[0]), :] = piece[...]
    for c in range(NCH):
        rows = slice(c * CH, (c + 1) * CH)
        mix_grad[rows, :] = dot(branch[rows, :], out_w[...], ((1,), (1,))).astype(BF)
    out_grad[...] = dot(mix[...], branch[...], ((0,), (0,))).astype(BF)


def branch_products(where, out_w, mix, pieces):
    shape = jax.ShapeDtypeStruct
    return pl.pallas_call(
        branch_kernel,
        out_shape=(shape((TOK, HW + HS), BF), shape((HW + HS, D), BF)),
        in_specs=[SMEM] + [VMEM] * 12,
        out_specs=(VMEM,) * 2,
        scratch_shapes=[pltpu.VMEM((TOK, D), BF)],
        compiler_params=PARAMS,
    )(where, out_w, mix, *pieces)


def mixer_backward(proj, small, y, states, log_totals, mix_grad):
    return pl.pallas_call(
        mixer_backward_kernel,
        out_shape=(jax.ShapeDtypeStruct((TOK, CW), BF), jax.ShapeDtypeStruct((8, 8), F32)),
        in_specs=[VMEM] * 6,
        out_specs=(VMEM,) * 2,
        scratch_shapes=[
            pltpu.VMEM((TOK, HS), BF),
            pltpu.VMEM((TOK, HS), BF),
            pltpu.VMEM((TOK, HS), F32),
            pltpu.VMEM((TOK, HS), F32),
        ],
        compiler_params=PARAMS,
    )(proj, small, y, states, log_totals, mix_grad)


def pack_weights_kernel(where, mixer_w, attn_w, gate_up, gains, out):
    half = ROWS // 2
    rows = pl.ds(pl.multiple_of(where[1] * half, half), half)
    g1, g2 = gains[rows, 0:1], gains[rows, 1:2]
    lane = lax.broadcasted_iota(jnp.int32, (MH, HS), 1)
    sub = lax.broadcasted_iota(jnp.int32, (MH, HS), 0)

    def part(ref, at, width, g):
        return (ref[rows, at : at + width].astype(F32) * g).astype(BF)

    both = part(mixer_w, 2 * INNER, 2 * NS, g1)
    steps_w = part(mixer_w, 2 * INNER + 2 * NS, MH, g1)
    for s in range(SEQ):
        head = s // (SEQ // KVH) * HS
        out[s, :, CB : CB + 2 * NS] = both
        out[s, :, CZ : CZ + HW] = part(mixer_w, s * HW, HW, g1)
        out[s, :, CQ : CQ + HS] = part(attn_w, s * HS, HS, g1)
        out[s, :, CU : CU + HW] = part(mixer_w, INNER + s * HW, HW, g1)
        out[s, :, CK : CK + HS] = part(attn_w, QH * HS + head, HS, g1)
        out[s, :, CV : CV + HS] = part(attn_w, (QH + KVH) * HS + head, HS, g1)
        own = ((sub == s * HL + lane) & (lane < HL)).astype(BF)
        out[s, :, CR:CW] = dot(steps_w, own).astype(BF)
        out[s, :, CW : CW + FL] = part(gate_up, s * FL, FL, g2)
        out[s, :, CW + FL :] = part(gate_up, FF + s * FL, FL, g2)


def pack_weights(where, mixer_w, attn_w, gate_up, gains):
    return pl.pallas_call(
        pack_weights_kernel,
        out_shape=jax.ShapeDtypeStruct((SEQ, ROWS // 2, CW + 2 * FL), BF),
        in_specs=[SMEM] + [VMEM] * 4,
        out_specs=VMEM,
        compiler_params=PARAMS,
    )(where, mixer_w, attn_w, gate_up, gains)


WM = 2 * INNER + 2 * NS + MH
WMP = 3456
WA = (QH + 2 * KVH) * HS


WA0 = WMP
WO0 = WMP + WA
WALL = WO0 + 2 * FF


def mixer_rows_kernel(got, got_gu, out, rows):
    for s in range(SEQ):
        rows[:, WO0 + s * 2 * FL : WO0 + (s + 1) * 2 * FL] = sum(
            got_gu[chip * SEQ + s].astype(F32) for chip in range(8)
        )
    share = [sum(got[chip * SEQ + s].astype(F32) for chip in range(8)) for s in range(SEQ)]
    lane = lax.broadcasted_iota(jnp.int32, (16, 128), 1)
    sub = lax.broadcasted_iota(jnp.int32, (16, 128), 0)
    tail = jnp.zeros((8, 128), F32)
    every = sum(share)
    for s in range(SEQ):
        rows[:, s * HW : (s + 1) * HW] = share[s][:, CZ : CZ + HW]
        rows[:, INNER + s * HW : INNER + (s + 1) * HW] = share[s][:, CU : CU + HW]
        rows[:, WA0 + s * HS : WA0 + (s + 1) * HS] = share[s][:, CQ : CQ + HS]
        place = ((lane == s * HL + sub) & (sub < HL)).astype(F32)
        tail = tail + dot(share[s][:, CR : CR + 16], place, precision=HIGH)
    rows[:, 2 * INNER : 2 * INNER + 2 * NS] = every[:, : 2 * NS]
    place = ((lane == MH - 8 + sub) & (sub >= 8)).astype(F32)
    tail = tail + dot(every[:, CR : CR + 16], place, precision=HIGH)
    place = ((lane == MH + 8 + sub) & (sub == 0)).astype(F32)
    tail = tail + dot(every[:, CR + 16 : CR + 32], place, precision=HIGH)
    rows[:, 2 * INNER + 2 * NS : WMP] = tail
    each = SEQ // KVH
    for j in range(KVH):
        both = sum(share[j * each : (j + 1) * each])
        at = WA0 + QH * HS + j * HS
        rows[:, at : at + HS] = both[:, CK : CK + HS]
        at = at + KVH * HS
        rows[:, at : at + HS] = both[:, CV : CV + HS]
    out[...] = rows[...].astype(BF)


def mixer_rows(got, got_gu):
    return pl.pallas_call(
        mixer_rows_kernel,
        out_shape=jax.ShapeDtypeStruct((8, WALL), BF),
        in_specs=[VMEM] * 2,
        out_specs=VMEM,
        scratch_shapes=[pltpu.VMEM((8, WALL), F32)],
        compiler_params=PARAMS,
    )(got, got_gu)


def finish_kernel(
    where, mine, other, mixer_w, attn_w, gate_up, gains, mixer_out, attn_out, gate_up_out, gain, line, rows
):
    half = ROWS // 2
    core = where[1]
    for source, at in ((mine, core * half), (other, half - core * half)):
        for i in range(half // 16):
            to = pl.ds(pl.multiple_of(at + i * 16, 16), 16)
            rows[to, :] = source[i * 16 : (i + 1) * 16, :].astype(F32)
    line[...] = rows[0:8, WM - MH : WMP] + rows[half : half + 8, WM - MH : WMP]
    for i in range(ROWS // 16):
        at = slice(i * 16, (i + 1) * 16)
        mixer, attn, g = rows[at, :WM], rows[at, WA0:WO0], gains[at, :]
        total = jnp.sum(mixer * mixer_w[at, :].astype(F32), axis=1, keepdims=True) + jnp.sum(
            attn * attn_w[at, :].astype(F32), axis=1, keepdims=True
        )
        mixer_out[at, :] = mixer * g[:, 0:1]
        attn_out[at, :] = attn * g[:, 0:1]
        total_two = jnp.zeros((16, 1), F32)
        for s in range(SEQ):
            for k in range(2):
                block = rows[at, WO0 + (s * 2 + k) * FL : WO0 + (s * 2 + k + 1) * FL]
                to = slice(k * FF + s * FL, k * FF + (s + 1) * FL)
                total_two = total_two + jnp.sum(
                    block * gate_up[at, to].astype(F32), axis=1, keepdims=True
                )
                gate_up_out[at, to] = block * g[:, 1:2]
        gain[at, :] = jnp.concatenate([total, total_two], axis=1)


def finish(where, mine, other, mixer_w, attn_w, gate_up, gains):
    shape = lambda *dims: jax.ShapeDtypeStruct(dims, F32)
    return pl.pallas_call(
        finish_kernel,
        out_shape=(
            shape(ROWS, WM), shape(ROWS, WA), shape(ROWS, 2 * FF), shape(ROWS, 2), shape(8, 128),
        ),
        in_specs=[SMEM] + [VMEM] * 6,
        out_specs=(VMEM,) * 5,
        scratch_shapes=[pltpu.VMEM((ROWS, WALL), F32)],
        compiler_params=PARAMS,
    )(where, mine, other, mixer_w, attn_w, gate_up, gains)


def unit_back(x, e):
    rho = lax.rsqrt(jnp.mean(x * x, axis=-1, keepdims=True) + EPS)
    return rho * e - x * (rho * rho * rho) * jnp.mean(x * e, axis=-1, keepdims=True)


def chip_groups():
    return [list(range(c, DP, 2)) for c in range(2)]


def core_sum(grad, core, line=None):
    n = grad.shape[1]
    parts = grad.reshape(SEQ, 2, ROWS // 2, n)
    mine = lax.dynamic_index_in_dim(parts, core, 1, False).astype(F32)
    other = core_swap(lax.dynamic_index_in_dim(parts, 1 - core, 1, False))
    both = mine + other.astype(F32)
    if line is not None:
        me = lax.axis_index("seq")
        here = (lax.broadcasted_iota(jnp.int32, both.shape, 0) == me) & (
            lax.broadcasted_iota(jnp.int32, both.shape, 1) == 0
        )
        both = both + jnp.where(here, line[None, None], 0.0)
    return both.astype(BF).reshape(SEQ, 8, 8, n).swapaxes(0, 1).reshape(64, 8, n)


def to_owners(sent):
    return lax.all_to_all(
        sent, ("dp", "seq"), split_axis=0, concat_axis=0, tiled=True, axis_index_groups=same_core()
    )


def local(
    inputs, cotangent, mixer_in, attn_in, mamba_out, attn_out, gate_up, down_proj,
    norm_gains, step_bias, decay_log, skip_gain,
):
    me = lax.axis_index("seq")
    core = lax.axis_index("dp") % 2
    where = jnp.stack([me, core]).astype(jnp.int32)
    x0 = inputs[0]
    gains = norm_gains[0].astype(F32).T
    down_w = down_proj[0]
    out_w = jnp.concatenate([mamba_out[0], attn_out[0]], axis=0)
    small = jnp.concatenate([step_bias, decay_log, skip_gain], axis=0).astype(F32)
    small = jnp.pad(small, ((0, 5), (0, 8 - HL)))

    pieces = gather_pieces(jnp.concatenate([x0, cotangent[0]], axis=1))
    w_mine = lax.all_to_all(
        pack_weights(where, mixer_in[0], attn_in[0], gate_up[0], gains),
        "seq", split_axis=0, concat_axis=0, tiled=True,
    )
    unit_one, ffn_grad, in_w, gu_w, proj, mix, y, states, log_totals, mid_part = mixer_forward(
        where, w_mine, core_swap(w_mine), small, out_w, pieces
    )
    mid, (act_grad,) = scatter_rows(
        mid_part, (dot(ffn_grad, down_w, ((1,), (1,))).astype(BF),)
    )
    mid = mid + x0.astype(F32)

    unit_two, act, up_grad, e_part = feed_forward(
        where, gu_w, act_grad, gather_pieces(unit_rows(mid).astype(BF))
    )
    gu_sent = core_sum(dot(unit_two, up_grad, ((0,), (0,))).astype(BF), core)
    down_grad = dot(act, ffn_grad, ((0,), (0,))).astype(BF)
    mid_e, (gu_sent, out_part, down_grad) = scatter_rows(
        e_part, (gu_sent, dot(act, down_w).astype(BF), down_grad)
    )
    mid_grad = cotangent[0].astype(F32) + unit_back(mid, mid_e)
    pieces = gather_pieces(mid_grad.astype(BF))
    *pieces, gu_got = lax.optimization_barrier((*pieces, to_owners(gu_sent)))

    mix_grad, out_grad = branch_products(where, out_w, mix, pieces)
    out_part, mix_grad = lax.optimization_barrier((out_part, mix_grad))
    proj_grad, sums = mixer_backward(proj, small, y, states, log_totals, mix_grad)
    row_sums = lax.psum(jnp.concatenate([down_grad, out_grad], axis=0), "dp")
    in_grad = dot(unit_one, proj_grad, ((0,), (0,))).astype(BF)
    line = jnp.concatenate([sums[0, :HL], sums[1, :HL], sums[2, :HL]])
    line = jnp.pad(line, (CR + 8, CW - CR - 8 - 3 * HL))
    e_part = dot(proj_grad, in_w, ((1,), (1,))).astype(BF)
    result, (sent, e_part) = scatter_rows(out_part, (core_sum(in_grad, core, line), e_part))
    outputs = (mid + result).astype(BF)
    rows = mixer_rows(to_owners(sent), gu_got)
    mine = lax.all_to_all(
        jnp.broadcast_to(rows[None], (8, 8, WALL)), "dp", split_axis=0, concat_axis=0, tiled=True,
        axis_index_groups=chip_groups(),
    ).reshape(ROWS // 2, WALL)
    in_e = scatter_rows_direct(e_part, me)
    input_grad = mid_grad + unit_back(x0.astype(F32), in_e)
    mixer_g, attn_g, gate_up_g, gain, line = finish(
        where, mine, core_swap(mine), mixer_in[0], attn_in[0], gate_up[0], gains
    )
    row_sums = row_sums.astype(F32)
    line = line[0:1, MH : MH + 3 * HL]
    return (
        outputs[None],
        input_grad[None],
        mixer_g[None],
        attn_g[None],
        row_sums[None, FL : FL + HW],
        row_sums[None, FL + HW :],
        gate_up_g[None],
        row_sums[None, :FL],
        gain.T[None],
        line[:, :HL],
        line[:, HL : 2 * HL],
        line[:, 2 * HL :],
    )


def solution(mesh):
    rows = P("dp", "seq", None)
    owned = P(None, "seq", None)
    heads = P(None, "seq")
    gains = P(None, None, "seq")
    return jax.shard_map(
        local,
        mesh=mesh,
        in_specs=(rows, rows) + (owned,) * 6 + (gains,) + (heads,) * 3,
        out_specs=(rows, rows) + (owned,) * 6 + (gains,) + (heads,) * 3,
        check_vma=False,
    )
```

```python
import jax
import jax.numpy as jnp
from jax import lax
from jax.experimental import pallas as pl
from jax.experimental.pallas import tpu as pltpu
from jax.sharding import PartitionSpec as P

MH = 24
MP = 64
NS = 128
QH = 8
KVH = 2
HS = 64
FF = 2048
SEQ = 8
DP = 16
HL = MH // SEQ
HW = HL * MP
INNER = MH * MP
FL = FF // SEQ
ROWS = 128
TOK = 1024
D = 1024
CH = 256
NCH = TOK // CH
CB, CC, CZ, CQ, CU, CK, CV, CR, CW = 0, 128, 256, 448, 512, 704, 768, 832, 896
EPS = 1e-05
NEG = -1e30
F32 = jnp.float32
BF = jnp.bfloat16
HIGH = lax.Precision.HIGHEST


def dot(a, b, dims=((1,), (0,)), precision=None):
    return lax.dot_general(a, b, (dims, ((), ())), precision=precision, preferred_element_type=F32)


def x_shift(k):
    return [(i, ((i // 2 + k) % 4) * 2 + i % 2) for i in range(SEQ)]


Z_SWAP = [(i, i ^ 1) for i in range(SEQ)]


PLACES = (
    (0, 0, 0), (0, 1, 0), (3, 0, 0), (1, 0, 0), (2, 0, 0), (2, 0, 64), (3, 1, 0), (1, 1, 0), (2, 1, 0), (2, 1, 64),
)


def gather_pieces(x):
    h = x.shape[0] // 2
    send = lambda v, perm: lax.ppermute(v, "seq", perm)
    z, a, b = send(x, Z_SWAP), send(x, x_shift(1)), send(x, x_shift(-1))
    c0, c1 = send(a[:h], x_shift(1)), send(b[h:], x_shift(-1))
    za, zb = send(z, x_shift(1)), send(z, x_shift(-1))
    zc0, zc1 = send(c0, Z_SWAP), send(c1, Z_SWAP)
    return x, z, a, b, c0, c1, za, zb, zc0, zc1


def gather_with_weights(x, packed):
    h = x.shape[0] // 2
    send = lambda v, perm: lax.ppermute(v, "seq", perm)
    z, a, b = send(x, Z_SWAP), send(x, x_shift(1)), send(x, x_shift(-1))
    z, packed = lax.optimization_barrier((z, packed))
    share = lax.all_to_all(packed, "seq", split_axis=0, concat_axis=0, tiled=True)
    shares = round_y(share)
    c0, c1 = send(a[:h], x_shift(1)), send(b[h:], x_shift(-1))
    za, zb = send(z, x_shift(1)), send(z, x_shift(-1))
    c0, c1, second = lax.optimization_barrier((c0, c1, shares[1]))
    shares = (shares[0], second, *shares[2:])
    zc = send(jnp.concatenate([c0, c1], axis=0), Z_SWAP)
    return (x, z, a, b, c0, c1, za, zb, zc), (*shares, *(core_swap(v) for v in shares))


def piece_row(me, place):
    dx, other, off = place
    mx, mz = me // 2, me % 2
    mz = 1 - mz if other else mz
    return pl.multiple_of(((mx + dx) % 4 * 2 + mz) * ROWS + off, 64)


def scatter_rows(part, beside=()):
    got = lax.all_to_all(part.reshape(SEQ, ROWS, D), "seq", split_axis=0, concat_axis=0, tiled=True)
    return lax.optimization_barrier((got, *beside))


def y_shift(v, k):
    return lax.ppermute(v, "dp", [(i, (i // 4 + k) % 4 * 4 + i % 4) for i in range(DP)])


def round_y(v):
    return v, y_shift(v, 3), y_shift(v, 2), y_shift(v, 1)


def core_swap(v):
    return lax.ppermute(v, "dp", [(i, i ^ 1) for i in range(DP)])


def same_core():
    return [[d * SEQ + s for d in range(c, DP, 2) for s in range(SEQ)] for c in range(2)]


def per_head(cols, shape):
    lane = lax.broadcasted_iota(jnp.int32, shape, 1)
    return jnp.where(lane < MP, cols[0], jnp.where(lane < 2 * MP, cols[1], cols[2]))


def widen(v8):
    return per_head([v8[:, h : h + 1] for h in range(HL)], (v8.shape[0], HW))


def row_heads(v8):
    row = lax.broadcasted_iota(jnp.int32, (HW, NS), 0)
    return jnp.where(row < MP, v8[:, 0:1], jnp.where(row < 2 * MP, v8[:, 1:2], v8[:, 2:3]))


def head_mask(h, shape):
    lane = lax.broadcasted_iota(jnp.int32, shape, 1)
    return (lane >= h * MP) & (lane < (h + 1) * MP)


def tri_lower():
    t = lax.broadcasted_iota(jnp.int32, (CH, CH), 0)
    s = lax.broadcasted_iota(jnp.int32, (CH, CH), 1)
    return t >= s


def steps(r8, small):
    pre = r8 + small[0:1, :]
    dt = jnp.log1p(jnp.exp(pre))
    return pre, dt, -jnp.exp(small[1:2, :]) * dt


def block_decays(log_decay):
    low = tri_lower()
    ones = low.astype(F32)
    cum = dot(ones, log_decay, precision=HIGH)
    cum_t = dot(log_decay, ones, ((0,), (1,)), precision=HIGH)
    decays = [
        jnp.exp(jnp.where(low, cum[:, h : h + 1] - cum_t[h : h + 1, :], NEG)) for h in range(HL)
    ]
    return cum, decays


def causal(c, scores):
    t = c * CH + lax.broadcasted_iota(jnp.int32, scores.shape, 0)
    s = lax.broadcasted_iota(jnp.int32, scores.shape, 1)
    return jnp.where(s <= t, scores, NEG)


def unit_rows(x):
    return x * lax.rsqrt(jnp.mean(x * x, axis=-1, keepdims=True) + EPS)


def mixer_forward_kernel(*refs):
    (
        where, small_ref, out_w, *pieces,
        unit, in_w, gu_w, proj, mix, y_out, states, log_totals, mid_part, keys, values,
    ) = refs
    me, core, y = where[0], where[1], where[2]
    shares, pieces = pieces[:8], pieces[8:]
    for piece, place in zip(pieces, PLACES):
        rows = pl.ds(piece_row(me, place), piece.shape[0])
        unit[rows, :] = unit_rows(piece[:, :D].astype(F32)).astype(BF)
    for k, share in enumerate(shares):
        from_core = core if k < 4 else 1 - core
        first = (y + k) % 4 * 32 + from_core * 16
        for j in range(SEQ):
            rows = pl.ds(pl.multiple_of(j * ROWS + first, 16), 16)
            in_w[rows, :] = share[j, :, :CW]
            gu_w[rows, :] = share[j, :, CW:]
    small = small_ref[...]
    state = jnp.zeros((HW, NS), F32)
    for c in range(NCH):
        rows = slice(c * CH, (c + 1) * CH)
        proj[rows, :] = dot(unit[rows, :], in_w[...])
        b = proj[rows, CB : CB + NS].astype(BF)
        cc = proj[rows, CC : CC + NS].astype(BF)
        z = proj[rows, CZ : CZ + HW]
        u = proj[rows, CU : CU + HW]
        _, dt, log_decay = steps(proj[rows, CR : CR + 8], small)
        cum, decays = block_decays(log_decay)
        g = dot(cc, b, ((1,), (1,)))
        v = u * widen(dt)
        vb = v.astype(BF)
        intra = [dot((m * g).astype(BF), vb) for m in decays]
        last = cum[CH - 1 : CH, :]
        y = per_head(intra, (CH, HW)) + widen(jnp.exp(cum)) * dot(
            cc, state.astype(BF), ((1,), (1,))
        )
        states[c] = state
        state = row_heads(jnp.exp(last)) * state + dot(
            (v * widen(jnp.exp(last - cum))).astype(BF), b, ((0,), (0,))
        )
        y = y + widen(jnp.broadcast_to(small[2:3, :], (CH, 8))) * u
        y_out[rows, :] = y
        mix[rows, 0:HW] = (y * z * jax.nn.sigmoid(z)).astype(BF)

        q = proj[rows, CQ : CQ + HS].astype(BF)
        keys[rows, :] = proj[rows, CK : CK + HS].astype(BF)
        values[rows, :] = proj[rows, CV : CV + HS].astype(BF)
        seen = (c + 1) * CH
        scores = causal(c, dot(q, keys[0:seen, :], ((1,), (1,))) * HS**-0.5)
        peak = jnp.max(scores, axis=1, keepdims=True)
        weights = jnp.exp(scores - peak)
        totals = jnp.sum(weights, axis=1, keepdims=True)
        probs = (weights / totals).astype(BF)
        mix[rows, HW : HW + HS] = dot(probs, values[0:seen, :]).astype(BF)
        log_totals[rows, :] = jnp.broadcast_to(peak + jnp.log(totals), (CH, 8))
        mid_part[rows, :] = dot(mix[rows, :], out_w[...]).astype(BF)


def mixer_backward_kernel(
    proj, small_ref, y_in, states, log_totals, mix_grad, out, sums, keys, values, key_grad, value_grad
):
    small = small_ref[...]
    skip_w = widen(jnp.broadcast_to(small[2:3, :], (CH, 8)))
    keys[...] = proj[:, CK : CK + HS].astype(BF)
    values[...] = proj[:, CV : CV + HS].astype(BF)
    key_grad[...] = jnp.zeros_like(key_grad)
    value_grad[...] = jnp.zeros_like(value_grad)
    state_grad = jnp.zeros((HW, NS), F32)
    low = tri_lower()
    ones_low = low.astype(F32)
    lane8 = lax.broadcasted_iota(jnp.int32, (HW, 8), 1)
    row8 = lax.broadcasted_iota(jnp.int32, (HW, 8), 0)
    heads = (row8 // MP == lane8).astype(BF)
    lane_ch = lax.broadcasted_iota(jnp.int32, (CH, 8), 1)
    lane_one = lax.broadcasted_iota(jnp.int32, (1, 8), 1)
    acc_bias = jnp.zeros((1, 8), F32)
    acc_decay = jnp.zeros((1, 8), F32)
    acc_skip = jnp.zeros((1, HW), F32)
    rate = jnp.exp(small[1:2, :])
    for c in reversed(range(NCH)):
        rows = slice(c * CH, (c + 1) * CH)
        seen = (c + 1) * CH
        q = proj[rows, CQ : CQ + HS].astype(BF)
        grad = mix_grad[rows, HW : HW + HS]
        scores = causal(c, dot(q, keys[0:seen, :], ((1,), (1,))) * HS**-0.5)
        probs = jnp.exp(scores - log_totals[rows, 0:1])
        prob_grad = dot(grad, values[0:seen, :], ((1,), (1,)))
        weighted = probs * prob_grad
        centre = jnp.sum(weighted, axis=1, keepdims=True)
        score_grad = (weighted - probs * centre).astype(BF)
        query_grad = dot(score_grad, keys[0:seen, :]) * HS**-0.5
        key_grad[0:seen, :] += dot(score_grad, q, ((0,), (0,)))
        value_grad[0:seen, :] += dot(probs.astype(BF), grad, ((0,), (0,)))
        out[rows, CQ : CQ + HS] = query_grad.astype(BF)
        out[rows, CK : CK + HS] = (key_grad[rows, :] * HS**-0.5).astype(BF)
        out[rows, CV : CV + HS] = value_grad[rows, :].astype(BF)

        b = proj[rows, CB : CB + NS].astype(BF)
        cc = proj[rows, CC : CC + NS].astype(BF)
        z = proj[rows, CZ : CZ + HW]
        u = proj[rows, CU : CU + HW]
        pre, dt, log_decay = steps(proj[rows, CR : CR + 8], small)
        cum, decays = block_decays(log_decay)
        last = cum[CH - 1 : CH, :]
        g = dot(cc, b, ((1,), (1,)))
        dt_w = widen(dt)
        v = u * dt_w
        vb = v.astype(BF)
        gated_grad = mix_grad[rows, 0:HW].astype(F32)
        gate = jax.nn.sigmoid(z)
        dy = gated_grad * z * gate
        out[rows, CZ : CZ + HW] = (
            gated_grad * y_in[rows, :] * gate * (1.0 + z * (1.0 - gate))
        ).astype(BF)
        dyb = dy.astype(BF)
        state = states[c]
        sb = state.astype(BF)
        qb = state_grad.astype(BF)
        grow = widen(jnp.exp(cum))
        fade = widen(jnp.exp(last - cum))
        v_grad_inter = fade * dot(b, qb, ((1,), (1,)))
        y_inter = grow * dot(cc, sb, ((1,), (1,)))
        g_grad = jnp.zeros((CH, CH), F32)
        v_grads = []
        cum_grad = jnp.zeros((CH, 8), F32)
        columns = []
        for h in range(HL):
            pair = dot(jnp.where(head_mask(h, (CH, HW)), dyb, jnp.zeros_like(dyb)), vb, ((1,), (1,)))
            mixed_pair = decays[h] * pair
            g_grad = g_grad + mixed_pair
            v_grads.append(dot((decays[h] * g).astype(BF), dyb, ((0,), (0,))))
            swing = mixed_pair * g
            cum_grad = cum_grad + jnp.where(
                lane_ch == h, jnp.sum(swing, axis=1, keepdims=True), 0.0
            )
            columns.append(jnp.sum(swing, axis=0, keepdims=True))
        cum_grad = cum_grad - jnp.concatenate(
            columns + [jnp.zeros((8 - HL, CH), F32)], axis=0
        ).T
        v_grad = per_head(v_grads, (CH, HW)) + v_grad_inter
        g_gradb = g_grad.astype(BF)
        grown = (grow * dy).astype(BF)
        out[rows, CC : CC + NS] = (dot(g_gradb, b) + dot(grown, sb)).astype(BF)
        out[rows, CB : CB + NS] = (
            dot(g_gradb, cc, ((0,), (0,))) + dot((fade * v).astype(BF), qb)
        ).astype(BF)
        out[rows, CU : CU + HW] = (skip_w * dy + dt_w * v_grad).astype(BF)
        both = state * state_grad
        over = jnp.zeros((1, 8), F32)
        for h in range(HL):
            one = jnp.sum(both[h * MP : (h + 1) * MP, :], axis=0, keepdims=True)
            over = over + jnp.where(lane_one == h, jnp.sum(one, axis=1, keepdims=True), 0.0)
        behind = dot((v * v_grad_inter).astype(BF), heads)
        ahead = cum_grad + dot((dy * y_inter).astype(BF), heads)
        decay_grad = (
            dot(ones_low, ahead, ((0,), (0,)), precision=HIGH)
            + dot(ones_low, behind, precision=HIGH)
            - behind
            + jnp.exp(last) * over
        )
        step_grad = dot((u * v_grad).astype(BF), heads) - rate * decay_grad
        r_grad = step_grad * jax.nn.sigmoid(pre)
        out[rows, CR : CR + HS] = jnp.concatenate(
            [r_grad, jnp.zeros((CH, HS - 8), F32)], axis=1
        ).astype(BF)
        acc_bias = acc_bias + jnp.sum(r_grad, axis=0, keepdims=True)
        acc_decay = acc_decay - rate * jnp.sum(dt * decay_grad, axis=0, keepdims=True)
        acc_skip = acc_skip + jnp.sum(dy * u, axis=0, keepdims=True)
        state_grad = row_heads(jnp.exp(last)) * state_grad + dot(grown, cc, ((0,), (0,)))
    skip_sum = jnp.zeros((1, 8), F32)
    for h in range(HL):
        one = jnp.sum(jnp.where(head_mask(h, (1, HW)), acc_skip, 0.0), axis=1, keepdims=True)
        skip_sum = skip_sum + jnp.where(lane_one == h, one, 0.0)
    sums[...] = jnp.concatenate([acc_bias, acc_decay, skip_sum, jnp.zeros((5, 8), F32)], axis=0)


VMEM = pl.BlockSpec(memory_space=pltpu.VMEM)
def cost(us):
    return pl.CostEstimate(flops=int(us * 1e9), bytes_accessed=1 << 20, transcendentals=0)


def params(mib):
    return pltpu.CompilerParams(vmem_limit_bytes=mib * 1024 * 1024)


SMEM = pl.BlockSpec(memory_space=pltpu.SMEM)


def mixer_forward(where, small, out_w, shares, pieces):
    shape = jax.ShapeDtypeStruct
    return pl.pallas_call(
        mixer_forward_kernel,
        out_shape=(
            shape((TOK, D), BF),
            shape((D, CW), BF),
            shape((D, 2 * FL), BF),
            shape((TOK, CW), F32),
            shape((TOK, HW + HS), BF),
            shape((TOK, HW), F32),
            shape((NCH, HW, NS), F32),
            shape((TOK, 8), F32),
            shape((TOK, D), BF),
        ),
        in_specs=[SMEM] + [VMEM] * 19,
        out_specs=(VMEM,) * 9,
        scratch_shapes=[pltpu.VMEM((TOK, HS), BF), pltpu.VMEM((TOK, HS), BF)],
        cost_estimate=cost(16),
        compiler_params=params(50),
    )(where, small, out_w, *shares, *pieces)


def feed_forward_kernel(*refs):
    where, gu_w, act_grad, *pieces, unit, act, up_grad, e_part = refs
    for piece, place in zip(pieces, PLACES):
        unit[pl.ds(piece_row(where[0], place), piece.shape[0]), :] = piece[...]
    for c in range(NCH):
        rows = slice(c * CH, (c + 1) * CH)
        gate_rows = dot(unit[rows, :], gu_w[...])
        gate, wide = gate_rows[:, :FL], gate_rows[:, FL:]
        s = jax.nn.sigmoid(gate)
        act[rows, :] = (gate * s * wide).astype(BF)
        grad = act_grad[rows, :].astype(F32)
        up_grad[rows, :FL] = (grad * wide * s * (1.0 + gate * (1.0 - s))).astype(BF)
        up_grad[rows, FL:] = (grad * gate * s).astype(BF)
        e_part[rows, :] = dot(up_grad[rows, :], gu_w[...], ((1,), (1,))).astype(BF)


def feed_forward(where, gu_w, act_grad, pieces):
    shape = jax.ShapeDtypeStruct
    return pl.pallas_call(
        feed_forward_kernel,
        out_shape=(
            shape((TOK, D), BF), shape((TOK, FL), BF), shape((TOK, 2 * FL), BF), shape((TOK, D), BF),
        ),
        in_specs=[SMEM] + [VMEM] * 12,
        out_specs=(VMEM,) * 4,
        cost_estimate=cost(6),
        compiler_params=params(50),
    )(where, gu_w, act_grad, *pieces)


def output_gradients_kernel(*refs):
    where, down_w, *pieces, ffn_grad, act_grad = refs
    for piece, place in zip(pieces, PLACES):
        ffn_grad[pl.ds(piece_row(where[0], place), piece.shape[0]), :] = piece[:, D:]
    for c in range(NCH):
        rows = slice(c * CH, (c + 1) * CH)
        act_grad[rows, :] = dot(ffn_grad[rows, :], down_w[...], ((1,), (1,))).astype(BF)


def output_gradients(where, down_w, pieces):
    shape = jax.ShapeDtypeStruct
    return pl.pallas_call(
        output_gradients_kernel,
        out_shape=(shape((TOK, D), BF), shape((TOK, FL), BF)),
        in_specs=[SMEM] + [VMEM] * 10,
        out_specs=(VMEM,) * 2,
        cost_estimate=cost(3),
        compiler_params=params(50),
    )(where, down_w, *pieces)


def branch_kernel(*refs):
    where, out_w, mix, *pieces, mix_grad, out_grad, branch = refs
    for piece, place in zip(pieces, PLACES):
        branch[pl.ds(piece_row(where[0], place), piece.shape[0]), :] = piece[...]
    for c in range(NCH):
        rows = slice(c * CH, (c + 1) * CH)
        mix_grad[rows, :] = dot(branch[rows, :], out_w[...], ((1,), (1,))).astype(BF)
    out_grad[...] = dot(mix[...], branch[...], ((0,), (0,))).astype(BF)


def branch_products(where, out_w, mix, pieces):
    shape = jax.ShapeDtypeStruct
    return pl.pallas_call(
        branch_kernel,
        out_shape=(shape((TOK, HW + HS), BF), shape((HW + HS, D), BF)),
        in_specs=[SMEM] + [VMEM] * 12,
        out_specs=(VMEM,) * 2,
        scratch_shapes=[pltpu.VMEM((TOK, D), BF)],
        cost_estimate=cost(3),
        compiler_params=params(50),
    )(where, out_w, mix, *pieces)


def mixer_backward(proj, small, y, states, log_totals, mix_grad):
    return pl.pallas_call(
        mixer_backward_kernel,
        out_shape=(jax.ShapeDtypeStruct((TOK, CW), BF), jax.ShapeDtypeStruct((8, 8), F32)),
        in_specs=[VMEM] * 6,
        out_specs=(VMEM,) * 2,
        scratch_shapes=[
            pltpu.VMEM((TOK, HS), BF),
            pltpu.VMEM((TOK, HS), BF),
            pltpu.VMEM((TOK, HS), F32),
            pltpu.VMEM((TOK, HS), F32),
        ],
        cost_estimate=cost(19),
        compiler_params=params(50),
    )(proj, small, y, states, log_totals, mix_grad)


def pack_weights_kernel(where, mixer_w, attn_w, gate_up, gains, out):
    rows = pl.ds(pl.multiple_of(where[2] * 32 + where[1] * 16, 16), 16)
    g1, g2 = gains[rows, 0:1], gains[rows, 1:2]
    lane = lax.broadcasted_iota(jnp.int32, (MH, HS), 1)
    sub = lax.broadcasted_iota(jnp.int32, (MH, HS), 0)

    def part(ref, at, width, g):
        return (ref[rows, at : at + width].astype(F32) * g).astype(BF)

    both = part(mixer_w, 2 * INNER, 2 * NS, g1)
    steps_w = part(mixer_w, 2 * INNER + 2 * NS, MH, g1)
    for s in range(SEQ):
        head = s // (SEQ // KVH) * HS
        out[s, :, CB : CB + 2 * NS] = both
        out[s, :, CZ : CZ + HW] = part(mixer_w, s * HW, HW, g1)
        out[s, :, CQ : CQ + HS] = part(attn_w, s * HS, HS, g1)
        out[s, :, CU : CU + HW] = part(mixer_w, INNER + s * HW, HW, g1)
        out[s, :, CK : CK + HS] = part(attn_w, QH * HS + head, HS, g1)
        out[s, :, CV : CV + HS] = part(attn_w, (QH + KVH) * HS + head, HS, g1)
        own = ((sub == s * HL + lane) & (lane < HL)).astype(BF)
        out[s, :, CR:CW] = dot(steps_w, own).astype(BF)
        out[s, :, CW : CW + FL] = part(gate_up, s * FL, FL, g2)
        out[s, :, CW + FL :] = part(gate_up, FF + s * FL, FL, g2)


def pack_weights(where, mixer_w, attn_w, gate_up, gains):
    return pl.pallas_call(
        pack_weights_kernel,
        out_shape=jax.ShapeDtypeStruct((SEQ, 16, CW + 2 * FL), BF),
        in_specs=[SMEM] + [VMEM] * 4,
        out_specs=VMEM,
        cost_estimate=cost(1),
        compiler_params=params(50),
    )(where, mixer_w, attn_w, gate_up, gains)


WM = 2 * INNER + 2 * NS + MH
WMP = 3456
WA = (QH + 2 * KVH) * HS


WA0 = WMP
WO0 = WMP + WA
WD0 = WO0 + 2 * FF
WALL = WD0 + 4 * D


def mixer_rows_kernel(got, got_gu, thin, out, rows):
    thin_rows = thin[...].astype(F32)
    for k in range(4):
        rows[:, WD0 + k * D : WD0 + (k + 1) * D] = thin_rows[k * 8 : (k + 1) * 8, :]
    for s in range(SEQ):
        rows[:, WO0 + s * 2 * FL : WO0 + (s + 1) * 2 * FL] = sum(
            got_gu[chip * SEQ + s].astype(F32) for chip in range(8)
        )
    share = [sum(got[chip * SEQ + s].astype(F32) for chip in range(8)) for s in range(SEQ)]
    lane = lax.broadcasted_iota(jnp.int32, (16, 128), 1)
    sub = lax.broadcasted_iota(jnp.int32, (16, 128), 0)
    tail = jnp.zeros((8, 128), F32)
    every = sum(share)
    for s in range(SEQ):
        rows[:, s * HW : (s + 1) * HW] = share[s][:, CZ : CZ + HW]
        rows[:, INNER + s * HW : INNER + (s + 1) * HW] = share[s][:, CU : CU + HW]
        rows[:, WA0 + s * HS : WA0 + (s + 1) * HS] = share[s][:, CQ : CQ + HS]
        place = ((lane == s * HL + sub) & (sub < HL)).astype(F32)
        tail = tail + dot(share[s][:, CR : CR + 16], place, precision=HIGH)
    rows[:, 2 * INNER : 2 * INNER + 2 * NS] = every[:, : 2 * NS]
    place = ((lane == MH - 8 + sub) & (sub >= 8)).astype(F32)
    tail = tail + dot(every[:, CR : CR + 16], place, precision=HIGH)
    place = ((lane == MH + 8 + sub) & (sub == 0)).astype(F32)
    tail = tail + dot(every[:, CR + 16 : CR + 32], place, precision=HIGH)
    rows[:, 2 * INNER + 2 * NS : WMP] = tail
    each = SEQ // KVH
    for j in range(KVH):
        both = sum(share[j * each : (j + 1) * each])
        at = WA0 + QH * HS + j * HS
        rows[:, at : at + HS] = both[:, CK : CK + HS]
        at = at + KVH * HS
        rows[:, at : at + HS] = both[:, CV : CV + HS]
    out[...] = rows[...].astype(BF)


def mixer_rows(got, got_gu, thin):
    return pl.pallas_call(
        mixer_rows_kernel,
        out_shape=jax.ShapeDtypeStruct((8, WALL), BF),
        in_specs=[VMEM] * 3,
        out_specs=VMEM,
        scratch_shapes=[pltpu.VMEM((8, WALL), F32)],
        cost_estimate=cost(1),
        compiler_params=params(50),
    )(got, got_gu, thin)


def finish_kernel(
    where, mixer_w, attn_w, gate_up, gains, *refs,
):
    blocks = refs[:8]
    (
    mixer_out, attn_out, gate_up_out, down_out, mamba_rows, attn_rows, gain, line, rows, thin,
    ) = refs[8:]
    core, y, high = where[1], where[2], where[3]
    half = ROWS // 2
    for n, block in enumerate(blocks):
        block = block[...].astype(F32)
        from_core, from_y = (core if n < 4 else 1 - core), (y + n) % 4
        for part in range(2):
            from_high = high if part == 0 else 1 - high
            source = block[part * 8 : (part + 1) * 8, :]
            to = pl.multiple_of(from_core * half + from_y * 16 + from_high * 8, 8)
            rows[pl.ds(to, 8), :] = source[:, :WD0]
            first = from_core * FL + from_y * 64 + from_high * 32
            for k in range(4):
                to = pl.multiple_of(first + k * 8, 8)
                thin[pl.ds(to, 8), :] = source[:, WD0 + k * D : WD0 + (k + 1) * D]
    down_out[...] = thin[:FL, :]
    mamba_rows[...] = thin[FL : FL + HW, :]
    attn_rows[...] = thin[FL + HW :, :]
    line[...] = rows[0:8, WM - MH : WMP] + rows[half : half + 8, WM - MH : WMP]
    for i in range(ROWS // 16):
        at = slice(i * 16, (i + 1) * 16)
        mixer, attn, g = rows[at, :WM], rows[at, WA0:WO0], gains[at, :]
        total = jnp.sum(mixer * mixer_w[at, :].astype(F32), axis=1, keepdims=True) + jnp.sum(
            attn * attn_w[at, :].astype(F32), axis=1, keepdims=True
        )
        rows[at, :WM] = mixer * g[:, 0:1]
        attn_out[at, :] = attn * g[:, 0:1]
        total_two = jnp.zeros((16, 1), F32)
        for s in range(SEQ):
            for k in range(2):
                block = rows[at, WO0 + (s * 2 + k) * FL : WO0 + (s * 2 + k + 1) * FL]
                to = slice(k * FF + s * FL, k * FF + (s + 1) * FL)
                total_two = total_two + jnp.sum(
                    block * gate_up[at, to].astype(F32), axis=1, keepdims=True
                )
                gate_up_out[at, to] = block * g[:, 1:2]
        gain[at, :] = jnp.concatenate([total, total_two], axis=1)
    for i in range(WMP // 128):
        n = min(128, WM - i * 128)
        mixer_out[i * 128 : i * 128 + n, :] = rows[:, i * 128 : (i + 1) * 128].T[:n, :]


def finish(where, mixer_w, attn_w, gate_up, gains, blocks):
    shape = lambda *dims: jax.ShapeDtypeStruct(dims, F32)
    return pl.pallas_call(
        finish_kernel,
        out_shape=(
            shape(WM, ROWS), shape(ROWS, WA), shape(ROWS, 2 * FF), shape(FL, D), shape(HW, D), shape(HS, D),
            shape(ROWS, 2), shape(8, 128),
        ),
        in_specs=[SMEM] + [VMEM] * 12,
        out_specs=(VMEM,) * 8,
        scratch_shapes=[pltpu.VMEM((ROWS, WD0), F32), pltpu.VMEM((2 * FL, D), F32)],
        cost_estimate=cost(6),
        compiler_params=params(32),
    )(where, mixer_w, attn_w, gate_up, gains, *blocks)


def unit_back(x, e):
    rho = lax.rsqrt(jnp.mean(x * x, axis=-1, keepdims=True) + EPS)
    return rho * e - x * (rho * rho * rho) * jnp.mean(x * e, axis=-1, keepdims=True)


def arrived(got, rows):
    return sum(got[k, rows, :].astype(F32) for k in range(SEQ))


def over_rows():
    return [slice(i * 16, (i + 1) * 16) for i in range(ROWS // 16)]


def mid_kernel(got, x, mid, unit):
    for rows in over_rows():
        value = x[rows, :].astype(F32) + arrived(got, rows)
        mid[rows, :] = value
        unit[rows, :] = unit_rows(value).astype(BF)


def mid_grad_kernel(got, cot, mid, grad, low):
    for rows in over_rows():
        value = cot[rows, :].astype(F32) + unit_back(mid[rows, :], arrived(got, rows))
        grad[rows, :] = value
        low[rows, :] = value.astype(BF)


def input_grad_kernel(got, x, mid_grad, grad):
    for rows in over_rows():
        grad[rows, :] = mid_grad[rows, :] + unit_back(x[rows, :].astype(F32), arrived(got, rows))


def output_kernel(got, mid, out):
    for rows in over_rows():
        out[rows, :] = (mid[rows, :] + arrived(got, rows)).astype(BF)


def on_rows(kernel, kinds, *arrays):
    return pl.pallas_call(
        kernel,
        out_shape=tuple(jax.ShapeDtypeStruct((ROWS, D), kind) for kind in kinds),
        in_specs=[VMEM] * len(arrays),
        out_specs=(VMEM,) * len(kinds),
        cost_estimate=cost(2),
        compiler_params=params(16),
    )(*arrays)


def core_sum(grad, core, line=None):
    n = grad.shape[1]
    parts = grad.reshape(SEQ, 2, ROWS // 2, n)
    mine = lax.dynamic_index_in_dim(parts, core, 1, False).astype(F32)
    other = core_swap(lax.dynamic_index_in_dim(parts, 1 - core, 1, False))
    both = mine + other.astype(F32)
    if line is not None:
        me = lax.axis_index("seq")
        here = (lax.broadcasted_iota(jnp.int32, both.shape, 0) == me) & (
            lax.broadcasted_iota(jnp.int32, both.shape, 1) == 0
        )
        both = both + jnp.where(here, line[None, None], 0.0)
    return both.astype(BF).reshape(SEQ, 8, 8, n).swapaxes(0, 1).reshape(64, 8, n)


def halved(v, mine, bit):
    v = v.reshape(2, v.shape[0] // 2, v.shape[1])
    other = lax.dynamic_index_in_dim(v, 1 - mine, 0, False)
    other = lax.ppermute(other, "dp", [(i, i ^ bit) for i in range(DP)])
    own = lax.dynamic_index_in_dim(v, mine, 0, False)
    return (own.astype(F32) + other.astype(F32)).astype(BF)


def to_owners(sent):
    return lax.all_to_all(
        sent, ("dp", "seq"), split_axis=0, concat_axis=0, tiled=True, axis_index_groups=same_core()
    )


def local(
    inputs, cotangent, mixer_in, attn_in, mamba_out, attn_out, gate_up, down_proj,
    norm_gains, step_bias, decay_log, skip_gain,
):
    me = lax.axis_index("seq")
    group = lax.axis_index("dp")
    core = group % 2
    high = group // 2 % 2
    where = jnp.stack([me, core, group // 4, high]).astype(jnp.int32)
    x0 = inputs[0]
    gains = norm_gains[0].astype(F32).T
    down_w = down_proj[0]
    out_w = jnp.concatenate([mamba_out[0], attn_out[0]], axis=0)
    small = jnp.concatenate([step_bias, decay_log, skip_gain], axis=0).astype(F32)
    small = jnp.pad(small, ((0, 5), (0, 8 - HL)))

    packed = pack_weights(where, mixer_in[0], attn_in[0], gate_up[0], gains)
    pieces, shares = gather_with_weights(jnp.concatenate([x0, cotangent[0]], axis=1), packed)
    unit_one, in_w, gu_w, proj, mix, y, states, log_totals, mid_part = mixer_forward(
        where, small, out_w, shares, pieces
    )
    ffn_grad, act_grad = output_gradients(where, down_w, pieces)
    got, ffn_grad, act_grad = scatter_rows(mid_part, (ffn_grad, act_grad))
    mid, unit_mid = on_rows(mid_kernel, (F32, BF), got, x0)

    unit_two, act, up_grad, e_part = feed_forward(
        where, gu_w, act_grad, gather_pieces(unit_mid)
    )
    gu_sent = core_sum(dot(unit_two, up_grad, ((0,), (0,))).astype(BF), core)
    down_grad = dot(act, ffn_grad, ((0,), (0,))).astype(BF)
    got, gu_sent, out_part, down_grad = scatter_rows(
        e_part, (gu_sent, dot(act, down_w).astype(BF), down_grad)
    )
    mid_grad, branch = on_rows(mid_grad_kernel, (F32, BF), got, cotangent[0], mid)
    pieces = gather_pieces(branch)
    *pieces, gu_got = lax.optimization_barrier((*pieces, to_owners(gu_sent)))

    mix_grad, out_grad = branch_products(where, out_w, mix, pieces)
    thin = halved(jnp.concatenate([down_grad, out_grad], axis=0), core, 1)
    mix_grad, out_part = lax.optimization_barrier((mix_grad, out_part))
    mix_grad, thin = lax.optimization_barrier((mix_grad, thin))
    proj_grad, sums = mixer_backward(proj, small, y, states, log_totals, mix_grad)
    proj_grad, thin = lax.optimization_barrier((proj_grad, halved(thin, group // 8, 8)))
    in_grad = dot(unit_one, proj_grad, ((0,), (0,))).astype(BF)
    thin = halved(thin, group // 4 % 2, 4)
    line = jnp.concatenate([sums[0, :HL], sums[1, :HL], sums[2, :HL]])
    line = jnp.pad(line, (CR + 8, CW - CR - 8 - 3 * HL))
    result, sent = scatter_rows(out_part, (core_sum(in_grad, core, line),))
    (outputs,) = on_rows(output_kernel, (BF,), result, mid)
    sent, proj_grad, thin = lax.optimization_barrier((sent, proj_grad, thin))
    e_part = dot(proj_grad, in_w, ((1,), (1,))).astype(BF)
    e_part, thin = lax.optimization_barrier((e_part, thin))
    thin = halved(thin, high, 2)
    got, outputs = lax.optimization_barrier((to_owners(sent), outputs))
    rows = mixer_rows(got, gu_got, thin)
    other_rows = lax.ppermute(rows, "dp", [(i, i ^ 2) for i in range(DP)])
    other_rows, e_part = lax.optimization_barrier((other_rows, e_part))
    blocks = round_y(jnp.concatenate([rows, other_rows], axis=0))
    blocks = (*blocks, *(core_swap(v) for v in blocks))
    (got,) = scatter_rows(e_part)
    (input_grad,) = on_rows(input_grad_kernel, (F32,), got, x0, mid_grad)
    mixer_g, attn_g, gate_up_g, down_g, mamba_out_g, attn_out_g, gain, line = finish(
        where, mixer_in[0], attn_in[0], gate_up[0], gains, blocks
    )
    line = line[0:1, MH : MH + 3 * HL]
    return (
        outputs[None],
        input_grad[None],
        mixer_g.T[None],
        attn_g[None],
        mamba_out_g[None],
        attn_out_g[None],
        gate_up_g[None],
        down_g[None],
        gain.T[None],
        line[:, :HL],
        line[:, HL : 2 * HL],
        line[:, 2 * HL :],
    )


def solution(mesh):
    rows = P("dp", "seq", None)
    owned = P(None, "seq", None)
    heads = P(None, "seq")
    gains = P(None, None, "seq")
    return jax.shard_map(
        local,
        mesh=mesh,
        in_specs=(rows, rows) + (owned,) * 6 + (gains,) + (heads,) * 3,
        out_specs=(rows, rows) + (owned,) * 6 + (gains,) + (heads,) * 3,
        check_vma=False,
    )
```

```python
import jax
import jax.numpy as jnp
from jax import lax
from jax.experimental import pallas as pl
from jax.experimental.pallas import tpu as pltpu
from jax.sharding import PartitionSpec as P

MH = 24
MP = 64
NS = 128
QH = 8
KVH = 2
HS = 64
FF = 2048
SEQ = 8
DP = 16
HL = MH // SEQ
HW = HL * MP
INNER = MH * MP
FL = FF // SEQ
ROWS = 128
TOK = 1024
D = 1024
CH = 256
NCH = TOK // CH
CB, CC, CZ, CQ, CU, CK, CV, CR, CW = 0, 128, 256, 448, 512, 704, 768, 832, 896
EPS = 1e-05
NEG = -1e30
F32 = jnp.float32
BF = jnp.bfloat16
HIGH = lax.Precision.HIGHEST


def dot(a, b, dims=((1,), (0,)), precision=None):
    return lax.dot_general(a, b, (dims, ((), ())), precision=precision, preferred_element_type=F32)


def x_shift(k):
    return [(i, ((i // 2 + k) % 4) * 2 + i % 2) for i in range(SEQ)]


Z_SWAP = [(i, i ^ 1) for i in range(SEQ)]


PLACES = (
    (0, 0, 0), (0, 1, 0), (3, 0, 0), (1, 0, 0), (2, 0, 0), (2, 0, 64), (3, 1, 0), (1, 1, 0), (2, 1, 0), (2, 1, 64),
)


def gather_pieces(x):
    h = x.shape[0] // 2
    send = lambda v, perm: lax.ppermute(v, "seq", perm)
    z, a, b = send(x, Z_SWAP), send(x, x_shift(1)), send(x, x_shift(-1))
    c0, c1 = send(a[:h], x_shift(1)), send(b[h:], x_shift(-1))
    za, zb = send(z, x_shift(1)), send(z, x_shift(-1))
    zc0, zc1 = send(c0, Z_SWAP), send(c1, Z_SWAP)
    return x, z, a, b, c0, c1, za, zb, zc0, zc1


def gather_with_weights(x, packed):
    h = x.shape[0] // 2
    send = lambda v, perm: lax.ppermute(v, "seq", perm)
    z, a, b = send(x, Z_SWAP), send(x, x_shift(1)), send(x, x_shift(-1))
    z, packed = lax.optimization_barrier((z, packed))
    share = lax.all_to_all(packed, "seq", split_axis=0, concat_axis=0, tiled=True)
    shares = round_y(share)
    c0, c1 = send(a[:h], x_shift(1)), send(b[h:], x_shift(-1))
    za, zb = send(z, x_shift(1)), send(z, x_shift(-1))
    c0, c1, second = lax.optimization_barrier((c0, c1, shares[1]))
    shares = (shares[0], second, *shares[2:])
    zc = send(jnp.concatenate([c0, c1], axis=0), Z_SWAP)
    return (x, z, a, b, c0, c1, za, zb, zc), (*shares, *(core_swap(v) for v in shares))


def piece_row(me, place):
    dx, other, off = place
    mx, mz = me // 2, me % 2
    mz = 1 - mz if other else mz
    return pl.multiple_of(((mx + dx) % 4 * 2 + mz) * ROWS + off, 64)


def scatter_rows(part, beside=()):
    got = lax.all_to_all(part.reshape(SEQ, ROWS, D), "seq", split_axis=0, concat_axis=0, tiled=True)
    return lax.optimization_barrier((got, *beside))


def y_shift(v, k):
    return lax.ppermute(v, "dp", [(i, (i // 4 + k) % 4 * 4 + i % 4) for i in range(DP)])


def round_y(v):
    return v, y_shift(v, 3), y_shift(v, 2), y_shift(v, 1)


def core_swap(v):
    return lax.ppermute(v, "dp", [(i, i ^ 1) for i in range(DP)])


def same_core():
    return [[d * SEQ + s for d in range(c, DP, 2) for s in range(SEQ)] for c in range(2)]


def per_head(cols, shape):
    lane = lax.broadcasted_iota(jnp.int32, shape, 1)
    return jnp.where(lane < MP, cols[0], jnp.where(lane < 2 * MP, cols[1], cols[2]))


def widen(v8):
    return per_head([v8[:, h : h + 1] for h in range(HL)], (v8.shape[0], HW))


def row_heads(v8):
    row = lax.broadcasted_iota(jnp.int32, (HW, NS), 0)
    return jnp.where(row < MP, v8[:, 0:1], jnp.where(row < 2 * MP, v8[:, 1:2], v8[:, 2:3]))


def head_mask(h, shape):
    lane = lax.broadcasted_iota(jnp.int32, shape, 1)
    return (lane >= h * MP) & (lane < (h + 1) * MP)


def tri_lower():
    t = lax.broadcasted_iota(jnp.int32, (CH, CH), 0)
    s = lax.broadcasted_iota(jnp.int32, (CH, CH), 1)
    return t >= s


def steps(r8, small):
    pre = r8 + small[0:1, :]
    dt = jnp.log1p(jnp.exp(pre))
    return pre, dt, -jnp.exp(small[1:2, :]) * dt


def block_decays(log_decay):
    low = tri_lower()
    ones = low.astype(F32)
    cum = dot(ones, log_decay, precision=HIGH)
    cum_t = dot(log_decay, ones, ((0,), (1,)), precision=HIGH)
    decays = [
        jnp.exp(jnp.where(low, cum[:, h : h + 1] - cum_t[h : h + 1, :], NEG)) for h in range(HL)
    ]
    return cum, decays


def causal(c, scores):
    t = c * CH + lax.broadcasted_iota(jnp.int32, scores.shape, 0)
    s = lax.broadcasted_iota(jnp.int32, scores.shape, 1)
    return jnp.where(s <= t, scores, NEG)


def unit_rows(x):
    return x * lax.rsqrt(jnp.mean(x * x, axis=-1, keepdims=True) + EPS)


def mixer_forward_kernel(*refs):
    (
        where, small_ref, out_w, *pieces,
        unit, in_w, gu_w, proj_out, steps_out, mix, y_out, states, log_totals, mid_part, keys, values, part,
    ) = refs
    me, core, y = where[0], where[1], where[2]
    shares, pieces = pieces[:8], pieces[8:]
    for piece, place in zip(pieces, PLACES):
        rows = pl.ds(piece_row(me, place), piece.shape[0])
        unit[rows, :] = unit_rows(piece[:, :D].astype(F32)).astype(BF)
    for k, share in enumerate(shares):
        from_core = core if k < 4 else 1 - core
        first = (y + k) % 4 * 32 + from_core * 16
        for j in range(SEQ):
            rows = pl.ds(pl.multiple_of(j * ROWS + first, 16), 16)
            in_w[rows, :] = share[j, :, :CW]
            gu_w[rows, :] = share[j, :, CW:]
    small = small_ref[...]
    state = jnp.zeros((HW, NS), F32)
    for c in range(NCH):
        rows = slice(c * CH, (c + 1) * CH)
        part[...] = dot(unit[rows, :], in_w[...])
        proj_out[rows, :] = part[...].astype(BF)
        steps_out[rows, :] = part[:, CR : CR + 8]
        b = part[:, CB : CB + NS].astype(BF)
        cc = part[:, CC : CC + NS].astype(BF)
        z = part[:, CZ : CZ + HW]
        u = part[:, CU : CU + HW]
        _, dt, log_decay = steps(part[:, CR : CR + 8], small)
        cum, decays = block_decays(log_decay)
        g = dot(cc, b, ((1,), (1,)))
        v = u * widen(dt)
        vb = v.astype(BF)
        intra = [dot((m * g).astype(BF), vb) for m in decays]
        last = cum[CH - 1 : CH, :]
        y = per_head(intra, (CH, HW)) + widen(jnp.exp(cum)) * dot(
            cc, state.astype(BF), ((1,), (1,))
        )
        states[c] = state
        state = row_heads(jnp.exp(last)) * state + dot(
            (v * widen(jnp.exp(last - cum))).astype(BF), b, ((0,), (0,))
        )
        y = y + widen(jnp.broadcast_to(small[2:3, :], (CH, 8))) * u
        y_out[rows, :] = y
        mix[rows, 0:HW] = (y * z * jax.nn.sigmoid(z)).astype(BF)

        q = part[:, CQ : CQ + HS].astype(BF)
        keys[rows, :] = part[:, CK : CK + HS].astype(BF)
        values[rows, :] = part[:, CV : CV + HS].astype(BF)
        seen = (c + 1) * CH
        scores = causal(c, dot(q, keys[0:seen, :], ((1,), (1,))) * HS**-0.5)
        peak = jnp.max(scores, axis=1, keepdims=True)
        weights = jnp.exp(scores - peak)
        totals = jnp.sum(weights, axis=1, keepdims=True)
        probs = (weights / totals).astype(BF)
        mix[rows, HW : HW + HS] = dot(probs, values[0:seen, :]).astype(BF)
        log_totals[rows, :] = jnp.broadcast_to(peak + jnp.log(totals), (CH, 8))
        mid_part[rows, :] = dot(mix[rows, :], out_w[...]).astype(BF)


def mixer_backward_kernel(
    proj, steps_in, small_ref, y_in, states, log_totals, mix_grad, out, sums, keys, values, key_grad, value_grad
):
    small = small_ref[...]
    skip_w = widen(jnp.broadcast_to(small[2:3, :], (CH, 8)))
    keys[...] = proj[:, CK : CK + HS].astype(BF)
    values[...] = proj[:, CV : CV + HS].astype(BF)
    key_grad[...] = jnp.zeros_like(key_grad)
    value_grad[...] = jnp.zeros_like(value_grad)
    state_grad = jnp.zeros((HW, NS), F32)
    low = tri_lower()
    ones_low = low.astype(F32)
    lane8 = lax.broadcasted_iota(jnp.int32, (HW, 8), 1)
    row8 = lax.broadcasted_iota(jnp.int32, (HW, 8), 0)
    heads = (row8 // MP == lane8).astype(BF)
    lane_ch = lax.broadcasted_iota(jnp.int32, (CH, 8), 1)
    lane_one = lax.broadcasted_iota(jnp.int32, (1, 8), 1)
    acc_bias = jnp.zeros((1, 8), F32)
    acc_decay = jnp.zeros((1, 8), F32)
    acc_skip = jnp.zeros((1, HW), F32)
    rate = jnp.exp(small[1:2, :])
    for c in reversed(range(NCH)):
        rows = slice(c * CH, (c + 1) * CH)
        seen = (c + 1) * CH
        q = proj[rows, CQ : CQ + HS].astype(BF)
        grad = mix_grad[rows, HW : HW + HS]
        scores = causal(c, dot(q, keys[0:seen, :], ((1,), (1,))) * HS**-0.5)
        probs = jnp.exp(scores - log_totals[rows, 0:1])
        prob_grad = dot(grad, values[0:seen, :], ((1,), (1,)))
        weighted = probs * prob_grad
        centre = jnp.sum(weighted, axis=1, keepdims=True)
        score_grad = (weighted - probs * centre).astype(BF)
        query_grad = dot(score_grad, keys[0:seen, :]) * HS**-0.5
        key_grad[0:seen, :] += dot(score_grad, q, ((0,), (0,)))
        value_grad[0:seen, :] += dot(probs.astype(BF), grad, ((0,), (0,)))
        out[rows, CQ : CQ + HS] = query_grad.astype(BF)
        out[rows, CK : CK + HS] = (key_grad[rows, :] * HS**-0.5).astype(BF)
        out[rows, CV : CV + HS] = value_grad[rows, :].astype(BF)

        b = proj[rows, CB : CB + NS].astype(BF)
        cc = proj[rows, CC : CC + NS].astype(BF)
        z = proj[rows, CZ : CZ + HW].astype(F32)
        u = proj[rows, CU : CU + HW].astype(F32)
        pre, dt, log_decay = steps(steps_in[rows, :], small)
        cum, decays = block_decays(log_decay)
        last = cum[CH - 1 : CH, :]
        g = dot(cc, b, ((1,), (1,)))
        dt_w = widen(dt)
        v = u * dt_w
        vb = v.astype(BF)
        gated_grad = mix_grad[rows, 0:HW].astype(F32)
        gate = jax.nn.sigmoid(z)
        dy = gated_grad * z * gate
        out[rows, CZ : CZ + HW] = (
            gated_grad * y_in[rows, :] * gate * (1.0 + z * (1.0 - gate))
        ).astype(BF)
        dyb = dy.astype(BF)
        state = states[c]
        sb = state.astype(BF)
        qb = state_grad.astype(BF)
        grow = widen(jnp.exp(cum))
        fade = widen(jnp.exp(last - cum))
        v_grad_inter = fade * dot(b, qb, ((1,), (1,)))
        y_inter = grow * dot(cc, sb, ((1,), (1,)))
        g_grad = jnp.zeros((CH, CH), F32)
        v_grads = []
        cum_grad = jnp.zeros((CH, 8), F32)
        columns = []
        for h in range(HL):
            pair = dot(jnp.where(head_mask(h, (CH, HW)), dyb, jnp.zeros_like(dyb)), vb, ((1,), (1,)))
            mixed_pair = decays[h] * pair
            g_grad = g_grad + mixed_pair
            v_grads.append(dot((decays[h] * g).astype(BF), dyb, ((0,), (0,))))
            swing = mixed_pair * g
            cum_grad = cum_grad + jnp.where(
                lane_ch == h, jnp.sum(swing, axis=1, keepdims=True), 0.0
            )
            columns.append(jnp.sum(swing, axis=0, keepdims=True))
        cum_grad = cum_grad - jnp.concatenate(
            columns + [jnp.zeros((8 - HL, CH), F32)], axis=0
        ).T
        v_grad = per_head(v_grads, (CH, HW)) + v_grad_inter
        g_gradb = g_grad.astype(BF)
        grown = (grow * dy).astype(BF)
        out[rows, CC : CC + NS] = (dot(g_gradb, b) + dot(grown, sb)).astype(BF)
        out[rows, CB : CB + NS] = (
            dot(g_gradb, cc, ((0,), (0,))) + dot((fade * v).astype(BF), qb)
        ).astype(BF)
        out[rows, CU : CU + HW] = (skip_w * dy + dt_w * v_grad).astype(BF)
        both = state * state_grad
        over = jnp.zeros((1, 8), F32)
        for h in range(HL):
            one = jnp.sum(both[h * MP : (h + 1) * MP, :], axis=0, keepdims=True)
            over = over + jnp.where(lane_one == h, jnp.sum(one, axis=1, keepdims=True), 0.0)
        behind = dot((v * v_grad_inter).astype(BF), heads)
        ahead = cum_grad + dot((dy * y_inter).astype(BF), heads)
        decay_grad = (
            dot(ones_low, ahead, ((0,), (0,)), precision=HIGH)
            + dot(ones_low, behind, precision=HIGH)
            - behind
            + jnp.exp(last) * over
        )
        step_grad = dot((u * v_grad).astype(BF), heads) - rate * decay_grad
        r_grad = step_grad * jax.nn.sigmoid(pre)
        out[rows, CR : CR + HS] = jnp.concatenate(
            [r_grad, jnp.zeros((CH, HS - 8), F32)], axis=1
        ).astype(BF)
        acc_bias = acc_bias + jnp.sum(r_grad, axis=0, keepdims=True)
        acc_decay = acc_decay - rate * jnp.sum(dt * decay_grad, axis=0, keepdims=True)
        acc_skip = acc_skip + jnp.sum(dy * u, axis=0, keepdims=True)
        state_grad = row_heads(jnp.exp(last)) * state_grad + dot(grown, cc, ((0,), (0,)))
    skip_sum = jnp.zeros((1, 8), F32)
    for h in range(HL):
        one = jnp.sum(jnp.where(head_mask(h, (1, HW)), acc_skip, 0.0), axis=1, keepdims=True)
        skip_sum = skip_sum + jnp.where(lane_one == h, one, 0.0)
    sums[...] = jnp.concatenate([acc_bias, acc_decay, skip_sum, jnp.zeros((5, 8), F32)], axis=0)


VMEM = pl.BlockSpec(memory_space=pltpu.VMEM)
def cost(us):
    return pl.CostEstimate(flops=int(us * 1e9), bytes_accessed=1 << 20, transcendentals=0)


def params(mib):
    return pltpu.CompilerParams(vmem_limit_bytes=mib * 1024 * 1024)


SMEM = pl.BlockSpec(memory_space=pltpu.SMEM)


def mixer_forward(where, small, out_w, shares, pieces):
    shape = jax.ShapeDtypeStruct
    return pl.pallas_call(
        mixer_forward_kernel,
        out_shape=(
            shape((TOK, D), BF),
            shape((D, CW), BF),
            shape((D, 2 * FL), BF),
            shape((TOK, CW), BF),
            shape((TOK, 8), F32),
            shape((TOK, HW + HS), BF),
            shape((TOK, HW), F32),
            shape((NCH, HW, NS), F32),
            shape((TOK, 8), F32),
            shape((TOK, D), BF),
        ),
        in_specs=[SMEM] + [VMEM] * 19,
        out_specs=(VMEM,) * 10,
        scratch_shapes=[pltpu.VMEM((TOK, HS), BF), pltpu.VMEM((TOK, HS), BF), pltpu.VMEM((CH, CW), F32)],
        cost_estimate=cost(16),
        compiler_params=params(50),
    )(where, small, out_w, *shares, *pieces)


def feed_forward_kernel(*refs):
    where, gu_w, act_grad, *pieces, unit, act, up_grad, e_part = refs
    for piece, place in zip(pieces, PLACES):
        unit[pl.ds(piece_row(where[0], place), piece.shape[0]), :] = piece[...]
    for c in range(NCH):
        rows = slice(c * CH, (c + 1) * CH)
        gate_rows = dot(unit[rows, :], gu_w[...])
        gate, wide = gate_rows[:, :FL], gate_rows[:, FL:]
        s = jax.nn.sigmoid(gate)
        act[rows, :] = (gate * s * wide).astype(BF)
        grad = act_grad[rows, :].astype(F32)
        up_grad[rows, :FL] = (grad * wide * s * (1.0 + gate * (1.0 - s))).astype(BF)
        up_grad[rows, FL:] = (grad * gate * s).astype(BF)
        e_part[rows, :] = dot(up_grad[rows, :], gu_w[...], ((1,), (1,))).astype(BF)


def feed_forward(where, gu_w, act_grad, pieces):
    shape = jax.ShapeDtypeStruct
    return pl.pallas_call(
        feed_forward_kernel,
        out_shape=(
            shape((TOK, D), BF), shape((TOK, FL), BF), shape((TOK, 2 * FL), BF), shape((TOK, D), BF),
        ),
        in_specs=[SMEM] + [VMEM] * 12,
        out_specs=(VMEM,) * 4,
        cost_estimate=cost(6),
        compiler_params=params(50),
    )(where, gu_w, act_grad, *pieces)


def output_gradients_kernel(*refs):
    where, down_w, *pieces, ffn_grad, act_grad = refs
    for piece, place in zip(pieces, PLACES):
        ffn_grad[pl.ds(piece_row(where[0], place), piece.shape[0]), :] = piece[:, D:]
    for c in range(NCH):
        rows = slice(c * CH, (c + 1) * CH)
        act_grad[rows, :] = dot(ffn_grad[rows, :], down_w[...], ((1,), (1,))).astype(BF)


def output_gradients(where, down_w, pieces):
    shape = jax.ShapeDtypeStruct
    return pl.pallas_call(
        output_gradients_kernel,
        out_shape=(shape((TOK, D), BF), shape((TOK, FL), BF)),
        in_specs=[SMEM] + [VMEM] * 10,
        out_specs=(VMEM,) * 2,
        cost_estimate=cost(3),
        compiler_params=params(50),
    )(where, down_w, *pieces)


def branch_kernel(*refs):
    where, out_w, mix, *pieces, mix_grad, out_grad, branch = refs
    for piece, place in zip(pieces, PLACES):
        branch[pl.ds(piece_row(where[0], place), piece.shape[0]), :] = piece[...]
    for c in range(NCH):
        rows = slice(c * CH, (c + 1) * CH)
        mix_grad[rows, :] = dot(branch[rows, :], out_w[...], ((1,), (1,))).astype(BF)
    out_grad[...] = dot(mix[...], branch[...], ((0,), (0,))).astype(BF)


def branch_products(where, out_w, mix, pieces):
    shape = jax.ShapeDtypeStruct
    return pl.pallas_call(
        branch_kernel,
        out_shape=(shape((TOK, HW + HS), BF), shape((HW + HS, D), BF)),
        in_specs=[SMEM] + [VMEM] * 12,
        out_specs=(VMEM,) * 2,
        scratch_shapes=[pltpu.VMEM((TOK, D), BF)],
        cost_estimate=cost(3),
        compiler_params=params(50),
    )(where, out_w, mix, *pieces)


def mixer_backward(proj, step_rows, small, y, states, log_totals, mix_grad):
    return pl.pallas_call(
        mixer_backward_kernel,
        out_shape=(jax.ShapeDtypeStruct((TOK, CW), BF), jax.ShapeDtypeStruct((8, 8), F32)),
        in_specs=[VMEM] * 7,
        out_specs=(VMEM,) * 2,
        scratch_shapes=[
            pltpu.VMEM((TOK, HS), BF),
            pltpu.VMEM((TOK, HS), BF),
            pltpu.VMEM((TOK, HS), F32),
            pltpu.VMEM((TOK, HS), F32),
        ],
        cost_estimate=cost(19),
        compiler_params=params(50),
    )(proj, step_rows, small, y, states, log_totals, mix_grad)


def pack_weights_kernel(where, mixer_w, attn_w, gate_up, gains, out):
    rows = pl.ds(pl.multiple_of(where[2] * 32 + where[1] * 16, 16), 16)
    g1, g2 = gains[rows, 0:1], gains[rows, 1:2]
    lane = lax.broadcasted_iota(jnp.int32, (MH, HS), 1)
    sub = lax.broadcasted_iota(jnp.int32, (MH, HS), 0)

    def part(ref, at, width, g):
        return (ref[rows, at : at + width].astype(F32) * g).astype(BF)

    both = part(mixer_w, 2 * INNER, 2 * NS, g1)
    steps_w = part(mixer_w, 2 * INNER + 2 * NS, MH, g1)
    for s in range(SEQ):
        head = s // (SEQ // KVH) * HS
        out[s, :, CB : CB + 2 * NS] = both
        out[s, :, CZ : CZ + HW] = part(mixer_w, s * HW, HW, g1)
        out[s, :, CQ : CQ + HS] = part(attn_w, s * HS, HS, g1)
        out[s, :, CU : CU + HW] = part(mixer_w, INNER + s * HW, HW, g1)
        out[s, :, CK : CK + HS] = part(attn_w, QH * HS + head, HS, g1)
        out[s, :, CV : CV + HS] = part(attn_w, (QH + KVH) * HS + head, HS, g1)
        own = ((sub == s * HL + lane) & (lane < HL)).astype(BF)
        out[s, :, CR:CW] = dot(steps_w, own).astype(BF)
        out[s, :, CW : CW + FL] = part(gate_up, s * FL, FL, g2)
        out[s, :, CW + FL :] = part(gate_up, FF + s * FL, FL, g2)


def pack_weights(where, mixer_w, attn_w, gate_up, gains):
    return pl.pallas_call(
        pack_weights_kernel,
        out_shape=jax.ShapeDtypeStruct((SEQ, 16, CW + 2 * FL), BF),
        in_specs=[SMEM] + [VMEM] * 4,
        out_specs=VMEM,
        cost_estimate=cost(1),
        compiler_params=params(50),
    )(where, mixer_w, attn_w, gate_up, gains)


WM = 2 * INNER + 2 * NS + MH
WMP = 3456
WA = (QH + 2 * KVH) * HS


WA0 = WMP
WO0 = WMP + WA
WD0 = WO0 + 2 * FF
WALL = WD0 + 4 * D


def mixer_rows_kernel(got, got_gu, thin, out, rows):
    thin_rows = thin[...].astype(F32)
    for k in range(4):
        rows[:, WD0 + k * D : WD0 + (k + 1) * D] = thin_rows[k * 8 : (k + 1) * 8, :]
    for s in range(SEQ):
        rows[:, WO0 + s * 2 * FL : WO0 + (s + 1) * 2 * FL] = sum(
            got_gu[chip * SEQ + s].astype(F32) for chip in range(8)
        )
    share = [sum(got[chip * SEQ + s].astype(F32) for chip in range(8)) for s in range(SEQ)]
    lane = lax.broadcasted_iota(jnp.int32, (16, 128), 1)
    sub = lax.broadcasted_iota(jnp.int32, (16, 128), 0)
    tail = jnp.zeros((8, 128), F32)
    every = sum(share)
    for s in range(SEQ):
        rows[:, s * HW : (s + 1) * HW] = share[s][:, CZ : CZ + HW]
        rows[:, INNER + s * HW : INNER + (s + 1) * HW] = share[s][:, CU : CU + HW]
        rows[:, WA0 + s * HS : WA0 + (s + 1) * HS] = share[s][:, CQ : CQ + HS]
        place = ((lane == s * HL + sub) & (sub < HL)).astype(F32)
        tail = tail + dot(share[s][:, CR : CR + 16], place, precision=HIGH)
    rows[:, 2 * INNER : 2 * INNER + 2 * NS] = every[:, : 2 * NS]
    place = ((lane == MH - 8 + sub) & (sub >= 8)).astype(F32)
    tail = tail + dot(every[:, CR : CR + 16], place, precision=HIGH)
    place = ((lane == MH + 8 + sub) & (sub == 0)).astype(F32)
    tail = tail + dot(every[:, CR + 16 : CR + 32], place, precision=HIGH)
    rows[:, 2 * INNER + 2 * NS : WMP] = tail
    each = SEQ // KVH
    for j in range(KVH):
        both = sum(share[j * each : (j + 1) * each])
        at = WA0 + QH * HS + j * HS
        rows[:, at : at + HS] = both[:, CK : CK + HS]
        at = at + KVH * HS
        rows[:, at : at + HS] = both[:, CV : CV + HS]
    out[...] = rows[...].astype(BF)


def mixer_rows(got, got_gu, thin):
    return pl.pallas_call(
        mixer_rows_kernel,
        out_shape=jax.ShapeDtypeStruct((8, WALL), BF),
        in_specs=[VMEM] * 3,
        out_specs=VMEM,
        scratch_shapes=[pltpu.VMEM((8, WALL), F32)],
        cost_estimate=cost(1),
        compiler_params=params(16),
    )(got, got_gu, thin)


def finish_kernel(
    where, mixer_w, attn_w, gate_up, gains, *refs,
):
    blocks = refs[:8]
    (
    mixer_out, attn_out, gate_up_out, down_out, mamba_rows, attn_rows, gain, line, rows, thin,
    ) = refs[8:]
    core, y, high = where[1], where[2], where[3]
    half = ROWS // 2
    for n, block in enumerate(blocks):
        block = block[...].astype(F32)
        from_core, from_y = (core if n < 4 else 1 - core), (y + n) % 4
        for part in range(2):
            from_high = high if part == 0 else 1 - high
            source = block[part * 8 : (part + 1) * 8, :]
            to = pl.multiple_of(from_core * half + from_y * 16 + from_high * 8, 8)
            rows[pl.ds(to, 8), :] = source[:, :WD0]
            first = from_core * FL + from_y * 64 + from_high * 32
            for k in range(4):
                to = pl.multiple_of(first + k * 8, 8)
                thin[pl.ds(to, 8), :] = source[:, WD0 + k * D : WD0 + (k + 1) * D]
    down_out[...] = thin[:FL, :]
    mamba_rows[...] = thin[FL : FL + HW, :]
    attn_rows[...] = thin[FL + HW :, :]
    line[...] = rows[0:8, WM - MH : WMP] + rows[half : half + 8, WM - MH : WMP]
    for i in range(ROWS // 16):
        at = slice(i * 16, (i + 1) * 16)
        mixer, attn, g = rows[at, :WM], rows[at, WA0:WO0], gains[at, :]
        total = jnp.sum(mixer * mixer_w[at, :].astype(F32), axis=1, keepdims=True) + jnp.sum(
            attn * attn_w[at, :].astype(F32), axis=1, keepdims=True
        )
        rows[at, :WM] = mixer * g[:, 0:1]
        attn_out[at, :] = attn * g[:, 0:1]
        total_two = jnp.zeros((16, 1), F32)
        for s in range(SEQ):
            for k in range(2):
                block = rows[at, WO0 + (s * 2 + k) * FL : WO0 + (s * 2 + k + 1) * FL]
                to = slice(k * FF + s * FL, k * FF + (s + 1) * FL)
                total_two = total_two + jnp.sum(
                    block * gate_up[at, to].astype(F32), axis=1, keepdims=True
                )
                gate_up_out[at, to] = block * g[:, 1:2]
        gain[at, :] = jnp.concatenate([total, total_two], axis=1)
    for i in range(WMP // 128):
        n = min(128, WM - i * 128)
        mixer_out[i * 128 : i * 128 + n, :] = rows[:, i * 128 : (i + 1) * 128].T[:n, :]


def finish(where, mixer_w, attn_w, gate_up, gains, blocks):
    shape = lambda *dims: jax.ShapeDtypeStruct(dims, F32)
    return pl.pallas_call(
        finish_kernel,
        out_shape=(
            shape(WM, ROWS), shape(ROWS, WA), shape(ROWS, 2 * FF), shape(FL, D), shape(HW, D), shape(HS, D),
            shape(ROWS, 2), shape(8, 128),
        ),
        in_specs=[SMEM] + [VMEM] * 12,
        out_specs=(VMEM,) * 8,
        scratch_shapes=[pltpu.VMEM((ROWS, WD0), F32), pltpu.VMEM((2 * FL, D), F32)],
        cost_estimate=cost(6),
        compiler_params=params(32),
    )(where, mixer_w, attn_w, gate_up, gains, *blocks)


def unit_back(x, e):
    rho = lax.rsqrt(jnp.mean(x * x, axis=-1, keepdims=True) + EPS)
    return rho * e - x * (rho * rho * rho) * jnp.mean(x * e, axis=-1, keepdims=True)


def arrived(got, rows):
    return sum(got[k, rows, :].astype(F32) for k in range(SEQ))


def over_rows():
    return [slice(i * 16, (i + 1) * 16) for i in range(ROWS // 16)]


def mid_kernel(got, x, mid, unit):
    for rows in over_rows():
        value = x[rows, :].astype(F32) + arrived(got, rows)
        mid[rows, :] = value
        unit[rows, :] = unit_rows(value).astype(BF)


def mid_grad_kernel(got, cot, mid, grad, low):
    for rows in over_rows():
        value = cot[rows, :].astype(F32) + unit_back(mid[rows, :], arrived(got, rows))
        grad[rows, :] = value
        low[rows, :] = value.astype(BF)


def input_grad_kernel(got, x, mid_grad, grad):
    for rows in over_rows():
        grad[rows, :] = mid_grad[rows, :] + unit_back(x[rows, :].astype(F32), arrived(got, rows))


def output_kernel(got, mid, out):
    for rows in over_rows():
        out[rows, :] = (mid[rows, :] + arrived(got, rows)).astype(BF)


def on_rows(kernel, kinds, *arrays):
    return pl.pallas_call(
        kernel,
        out_shape=tuple(jax.ShapeDtypeStruct((ROWS, D), kind) for kind in kinds),
        in_specs=[VMEM] * len(arrays),
        out_specs=(VMEM,) * len(kinds),
        cost_estimate=cost(2),
        compiler_params=params(16),
    )(*arrays)


def core_sum(grad, core):
    n = grad.shape[1]
    parts = grad.reshape(SEQ, 2, ROWS // 2, n)
    mine = lax.dynamic_index_in_dim(parts, core, 1, False).astype(F32)
    other = core_swap(lax.dynamic_index_in_dim(parts, 1 - core, 1, False))
    both = mine + other.astype(F32)
    return both.astype(BF).reshape(SEQ, 8, 8, n).swapaxes(0, 1).reshape(64, 8, n)


def core_sum_kernel(where, mine, other, line, out):
    first = lax.broadcasted_iota(jnp.int32, (ROWS // 2, CW), 0) == 0
    for j in range(SEQ):
        value = mine[j].astype(F32) + other[j].astype(F32)
        value = value + jnp.where(first & (where[0] == j), line[0:1, :], 0.0)
        for chip in range(8):
            out[chip * SEQ + j] = value[chip * 8 : (chip + 1) * 8, :].astype(BF)


def core_sum_with(where, in_grad, line, core):
    parts = in_grad.reshape(SEQ, 2, ROWS // 2, CW)
    other = core_swap(lax.dynamic_index_in_dim(parts, 1 - core, 1, False))
    mine = lax.dynamic_index_in_dim(parts, core, 1, False)
    return pl.pallas_call(
        core_sum_kernel,
        out_shape=jax.ShapeDtypeStruct((64, 8, CW), BF),
        in_specs=[SMEM] + [VMEM] * 3,
        out_specs=VMEM,
        cost_estimate=cost(1),
        compiler_params=params(16),
    )(where, mine, other, line)


def halved(v, mine, bit):
    v = v.reshape(2, v.shape[0] // 2, v.shape[1])
    other = lax.dynamic_index_in_dim(v, 1 - mine, 0, False)
    other = lax.ppermute(other, "dp", [(i, i ^ bit) for i in range(DP)])
    own = lax.dynamic_index_in_dim(v, mine, 0, False)
    return (own.astype(F32) + other.astype(F32)).astype(BF)


def to_owners(sent):
    return lax.all_to_all(
        sent, ("dp", "seq"), split_axis=0, concat_axis=0, tiled=True, axis_index_groups=same_core()
    )


def local(
    inputs, cotangent, mixer_in, attn_in, mamba_out, attn_out, gate_up, down_proj,
    norm_gains, step_bias, decay_log, skip_gain,
):
    me = lax.axis_index("seq")
    group = lax.axis_index("dp")
    core = group % 2
    high = group // 2 % 2
    where = jnp.stack([me, core, group // 4, high]).astype(jnp.int32)
    x0 = inputs[0]
    gains = norm_gains[0].astype(F32).T
    down_w = down_proj[0]
    out_w = jnp.concatenate([mamba_out[0], attn_out[0]], axis=0)
    small = jnp.concatenate([step_bias, decay_log, skip_gain], axis=0).astype(F32)
    small = jnp.pad(small, ((0, 5), (0, 8 - HL)))

    packed = pack_weights(where, mixer_in[0], attn_in[0], gate_up[0], gains)
    pieces, shares = gather_with_weights(jnp.concatenate([x0, cotangent[0]], axis=1), packed)
    unit_one, in_w, gu_w, proj, step_rows, mix, y, states, log_totals, mid_part = mixer_forward(
        where, small, out_w, shares, pieces
    )
    ffn_grad, act_grad = output_gradients(where, down_w, pieces)
    got, ffn_grad, act_grad = scatter_rows(mid_part, (ffn_grad, act_grad))
    mid, unit_mid = on_rows(mid_kernel, (F32, BF), got, x0)

    unit_two, act, up_grad, e_part = feed_forward(
        where, gu_w, act_grad, gather_pieces(unit_mid)
    )
    gu_sent = core_sum(dot(unit_two, up_grad, ((0,), (0,))).astype(BF), core)
    down_grad = dot(act, ffn_grad, ((0,), (0,))).astype(BF)
    got, gu_sent, out_part, down_grad = scatter_rows(
        e_part, (gu_sent, dot(act, down_w).astype(BF), down_grad)
    )
    mid_grad, branch = on_rows(mid_grad_kernel, (F32, BF), got, cotangent[0], mid)
    pieces = gather_pieces(branch)
    *pieces, gu_got = lax.optimization_barrier((*pieces, to_owners(gu_sent)))

    mix_grad, out_grad = branch_products(where, out_w, mix, pieces)
    kept = core_swap(jnp.where(core == 0, out_grad, down_grad))
    mix_grad, out_part = lax.optimization_barrier((mix_grad, out_part))
    thin = jnp.where(core == 0, down_grad, out_grad).astype(F32) + kept.astype(F32)
    mix_grad, thin = lax.optimization_barrier((mix_grad, thin.astype(BF)))
    proj_grad, sums = mixer_backward(proj, step_rows, small, y, states, log_totals, mix_grad)
    proj_grad, thin = lax.optimization_barrier((proj_grad, halved(thin, group // 8, 8)))
    in_grad = dot(unit_one, proj_grad, ((0,), (0,))).astype(BF)
    line = jnp.concatenate([sums[0, :HL], sums[1, :HL], sums[2, :HL]])
    line = jnp.pad(line, (CR + 8, CW - CR - 8 - 3 * HL))
    line = jnp.broadcast_to(line[None], (8, CW))
    result, sent = scatter_rows(out_part, (core_sum_with(where, in_grad, line, core),))
    (outputs,) = on_rows(output_kernel, (BF,), result, mid)
    sent, proj_grad, thin = lax.optimization_barrier((sent, proj_grad, thin))
    e_part = dot(proj_grad, in_w, ((1,), (1,))).astype(BF)
    e_part, thin = lax.optimization_barrier((e_part, halved(thin, group // 4 % 2, 4)))
    thin = halved(thin, high, 2)
    got, outputs = lax.optimization_barrier((to_owners(sent), outputs))
    rows = mixer_rows(got, gu_got, thin)
    other_rows = lax.ppermute(rows, "dp", [(i, i ^ 2) for i in range(DP)])
    other_rows, e_part = lax.optimization_barrier((other_rows, e_part))
    blocks = round_y(jnp.concatenate([rows, other_rows], axis=0))
    blocks = (*blocks, *(core_swap(v) for v in blocks))
    (got,) = scatter_rows(e_part)
    (input_grad,) = on_rows(input_grad_kernel, (F32,), got, x0, mid_grad)
    mixer_g, attn_g, gate_up_g, down_g, mamba_out_g, attn_out_g, gain, line = finish(
        where, mixer_in[0], attn_in[0], gate_up[0], gains, blocks
    )
    line = line[0:1, MH : MH + 3 * HL]
    return (
        outputs[None],
        input_grad[None],
        mixer_g.T[None],
        attn_g[None],
        mamba_out_g[None],
        attn_out_g[None],
        gate_up_g[None],
        down_g[None],
        gain.T[None],
        line[:, :HL],
        line[:, HL : 2 * HL],
        line[:, 2 * HL :],
    )


def solution(mesh):
    rows = P("dp", "seq", None)
    owned = P(None, "seq", None)
    heads = P(None, "seq")
    gains = P(None, None, "seq")
    return jax.shard_map(
        local,
        mesh=mesh,
        in_specs=(rows, rows) + (owned,) * 6 + (gains,) + (heads,) * 3,
        out_specs=(rows, rows) + (owned,) * 6 + (gains,) + (heads,) * 3,
        check_vma=False,
    )
```

```python
import jax
import jax.numpy as jnp
from jax import lax
from jax.experimental import pallas as pl
from jax.experimental.pallas import tpu as pltpu
from jax.sharding import PartitionSpec as P

MH = 24
MP = 64
NS = 128
QH = 8
KVH = 2
HS = 64
FF = 2048
SEQ = 8
DP = 16
HL = MH // SEQ
HW = HL * MP
INNER = MH * MP
FL = FF // SEQ
ROWS = 128
TOK = 1024
D = 1024
CH = 256
NCH = TOK // CH
CB, CC, CZ, CQ, CU, CK, CV, CR, CW = 0, 128, 256, 448, 512, 704, 768, 832, 896
EPS = 1e-05
NEG = -1e30
F32 = jnp.float32
BF = jnp.bfloat16
HIGH = lax.Precision.HIGHEST


def dot(a, b, dims=((1,), (0,)), precision=None):
    return lax.dot_general(a, b, (dims, ((), ())), precision=precision, preferred_element_type=F32)


def x_shift(k):
    return [(i, ((i // 2 + k) % 4) * 2 + i % 2) for i in range(SEQ)]


Z_SWAP = [(i, i ^ 1) for i in range(SEQ)]


PLACES = (
    (0, 0, 0), (0, 1, 0), (3, 0, 0), (1, 0, 0), (2, 0, 0), (2, 0, 64), (3, 1, 0), (1, 1, 0), (2, 1, 0), (2, 1, 64),
)


def gather_pieces(x):
    h = x.shape[0] // 2
    send = lambda v, perm: lax.ppermute(v, "seq", perm)
    z, a, b = send(x, Z_SWAP), send(x, x_shift(1)), send(x, x_shift(-1))
    c0, c1 = send(a[:h], x_shift(1)), send(b[h:], x_shift(-1))
    za, zb = send(z, x_shift(1)), send(z, x_shift(-1))
    zc0, zc1 = send(c0, Z_SWAP), send(c1, Z_SWAP)
    return x, z, a, b, c0, c1, za, zb, zc0, zc1


def gather_with_weights(x, packed):
    h = x.shape[0] // 2
    send = lambda v, perm: lax.ppermute(v, "seq", perm)
    z, a, b = send(x, Z_SWAP), send(x, x_shift(1)), send(x, x_shift(-1))
    z, packed = lax.optimization_barrier((z, packed))
    share = lax.all_to_all(packed, "seq", split_axis=0, concat_axis=0, tiled=True)
    shares = round_y(share)
    c0, c1 = send(a[:h], x_shift(1)), send(b[h:], x_shift(-1))
    za, zb = send(z, x_shift(1)), send(z, x_shift(-1))
    c0, c1, second = lax.optimization_barrier((c0, c1, shares[1]))
    shares = (shares[0], second, *shares[2:])
    zc = send(jnp.concatenate([c0, c1], axis=0), Z_SWAP)
    return (x, z, a, b, c0, c1, za, zb, zc), (*shares, *(core_swap(v) for v in shares))


def piece_row(me, place):
    dx, other, off = place
    mx, mz = me // 2, me % 2
    mz = 1 - mz if other else mz
    return pl.multiple_of(((mx + dx) % 4 * 2 + mz) * ROWS + off, 64)


def scatter_rows(part, beside=()):
    got = lax.all_to_all(part.reshape(SEQ, ROWS, D), "seq", split_axis=0, concat_axis=0, tiled=True)
    return lax.optimization_barrier((got, *beside))


def y_shift(v, k):
    return lax.ppermute(v, "dp", [(i, (i // 4 + k) % 4 * 4 + i % 4) for i in range(DP)])


def round_y(v):
    return v, y_shift(v, 3), y_shift(v, 2), y_shift(v, 1)


def core_swap(v):
    return lax.ppermute(v, "dp", [(i, i ^ 1) for i in range(DP)])


def same_core():
    return [[d * SEQ + s for d in range(c, DP, 2) for s in range(SEQ)] for c in range(2)]


def per_head(cols, shape):
    lane = lax.broadcasted_iota(jnp.int32, shape, 1)
    return jnp.where(lane < MP, cols[0], jnp.where(lane < 2 * MP, cols[1], cols[2]))


def widen(v8):
    return per_head([v8[:, h : h + 1] for h in range(HL)], (v8.shape[0], HW))


def row_heads(v8):
    row = lax.broadcasted_iota(jnp.int32, (HW, NS), 0)
    return jnp.where(row < MP, v8[:, 0:1], jnp.where(row < 2 * MP, v8[:, 1:2], v8[:, 2:3]))


def head_mask(h, shape):
    lane = lax.broadcasted_iota(jnp.int32, shape, 1)
    return (lane >= h * MP) & (lane < (h + 1) * MP)


def tri_lower():
    t = lax.broadcasted_iota(jnp.int32, (CH, CH), 0)
    s = lax.broadcasted_iota(jnp.int32, (CH, CH), 1)
    return t >= s


def steps(r8, small):
    pre = r8 + small[0:1, :]
    dt = jnp.log1p(jnp.exp(pre))
    return pre, dt, -jnp.exp(small[1:2, :]) * dt


def block_decays(log_decay):
    low = tri_lower()
    ones = low.astype(F32)
    cum = dot(ones, log_decay, precision=HIGH)
    cum_t = dot(log_decay, ones, ((0,), (1,)), precision=HIGH)
    decays = [
        jnp.exp(jnp.where(low, cum[:, h : h + 1] - cum_t[h : h + 1, :], NEG)) for h in range(HL)
    ]
    return cum, decays


def causal(c, scores):
    t = c * CH + lax.broadcasted_iota(jnp.int32, scores.shape, 0)
    s = lax.broadcasted_iota(jnp.int32, scores.shape, 1)
    return jnp.where(s <= t, scores, NEG)


def unit_rows(x):
    return x * lax.rsqrt(jnp.mean(x * x, axis=-1, keepdims=True) + EPS)


def mixer_forward_kernel(*refs):
    (
        where, small_ref, out_w, *pieces,
        unit, in_w, gu_w, proj_out, steps_out, mix, y_out, states, log_totals, mid_part, keys, values, part,
    ) = refs
    me, core, y = where[0], where[1], where[2]
    shares, pieces = pieces[:8], pieces[8:]
    for piece, place in zip(pieces, PLACES):
        rows = pl.ds(piece_row(me, place), piece.shape[0])
        unit[rows, :] = unit_rows(piece[:, :D].astype(F32)).astype(BF)
    for k, share in enumerate(shares):
        from_core = core if k < 4 else 1 - core
        first = (y + k) % 4 * 32 + from_core * 16
        for j in range(SEQ):
            rows = pl.ds(pl.multiple_of(j * ROWS + first, 16), 16)
            in_w[rows, :] = share[j, :, :CW]
            gu_w[rows, :] = share[j, :, CW:]
    small = small_ref[...]
    state = jnp.zeros((HW, NS), F32)
    for c in range(NCH):
        rows = slice(c * CH, (c + 1) * CH)
        part[...] = dot(unit[rows, :], in_w[...])
        proj_out[rows, :] = part[...].astype(BF)
        steps_out[rows, :] = part[:, CR : CR + 8]
        b = part[:, CB : CB + NS].astype(BF)
        cc = part[:, CC : CC + NS].astype(BF)
        z = part[:, CZ : CZ + HW]
        u = part[:, CU : CU + HW]
        _, dt, log_decay = steps(part[:, CR : CR + 8], small)
        cum, decays = block_decays(log_decay)
        g = dot(cc, b, ((1,), (1,)))
        v = u * widen(dt)
        vb = v.astype(BF)
        intra = [dot((m * g).astype(BF), vb) for m in decays]
        last = cum[CH - 1 : CH, :]
        y = per_head(intra, (CH, HW)) + widen(jnp.exp(cum)) * dot(
            cc, state.astype(BF), ((1,), (1,))
        )
        states[c] = state
        state = row_heads(jnp.exp(last)) * state + dot(
            (v * widen(jnp.exp(last - cum))).astype(BF), b, ((0,), (0,))
        )
        y = y + widen(jnp.broadcast_to(small[2:3, :], (CH, 8))) * u
        y_out[rows, :] = y
        mix[rows, 0:HW] = (y * z * jax.nn.sigmoid(z)).astype(BF)

        q = part[:, CQ : CQ + HS].astype(BF)
        keys[rows, :] = part[:, CK : CK + HS].astype(BF)
        values[rows, :] = part[:, CV : CV + HS].astype(BF)
        seen = (c + 1) * CH
        scores = causal(c, dot(q, keys[0:seen, :], ((1,), (1,))) * HS**-0.5)
        peak = jnp.max(scores, axis=1, keepdims=True)
        weights = jnp.exp(scores - peak)
        totals = jnp.sum(weights, axis=1, keepdims=True)
        probs = (weights / totals).astype(BF)
        mix[rows, HW : HW + HS] = dot(probs, values[0:seen, :]).astype(BF)
        log_totals[rows, :] = jnp.broadcast_to(peak + jnp.log(totals), (CH, 8))
        mid_part[rows, :] = dot(mix[rows, :], out_w[...]).astype(BF)


def mixer_backward_kernel(
    proj, steps_in, small_ref, y_in, states, log_totals, mix_grad, out, sums, keys, values, key_grad, value_grad
):
    small = small_ref[...]
    skip_w = widen(jnp.broadcast_to(small[2:3, :], (CH, 8)))
    keys[...] = proj[:, CK : CK + HS].astype(BF)
    values[...] = proj[:, CV : CV + HS].astype(BF)
    key_grad[...] = jnp.zeros_like(key_grad)
    value_grad[...] = jnp.zeros_like(value_grad)
    state_grad = jnp.zeros((HW, NS), F32)
    low = tri_lower()
    ones_low = low.astype(F32)
    lane8 = lax.broadcasted_iota(jnp.int32, (HW, 8), 1)
    row8 = lax.broadcasted_iota(jnp.int32, (HW, 8), 0)
    heads = (row8 // MP == lane8).astype(BF)
    lane_ch = lax.broadcasted_iota(jnp.int32, (CH, 8), 1)
    lane_one = lax.broadcasted_iota(jnp.int32, (1, 8), 1)
    acc_bias = jnp.zeros((1, 8), F32)
    acc_decay = jnp.zeros((1, 8), F32)
    acc_skip = jnp.zeros((1, HW), F32)
    rate = jnp.exp(small[1:2, :])
    for c in reversed(range(NCH)):
        rows = slice(c * CH, (c + 1) * CH)
        seen = (c + 1) * CH
        q = proj[rows, CQ : CQ + HS].astype(BF)
        grad = mix_grad[rows, HW : HW + HS]
        scores = causal(c, dot(q, keys[0:seen, :], ((1,), (1,))) * HS**-0.5)
        probs = jnp.exp(scores - log_totals[rows, 0:1])
        prob_grad = dot(grad, values[0:seen, :], ((1,), (1,)))
        weighted = probs * prob_grad
        centre = jnp.sum(weighted, axis=1, keepdims=True)
        score_grad = (weighted - probs * centre).astype(BF)
        query_grad = dot(score_grad, keys[0:seen, :]) * HS**-0.5
        key_grad[0:seen, :] += dot(score_grad, q, ((0,), (0,)))
        value_grad[0:seen, :] += dot(probs.astype(BF), grad, ((0,), (0,)))
        out[rows, CQ : CQ + HS] = query_grad.astype(BF)
        out[rows, CK : CK + HS] = (key_grad[rows, :] * HS**-0.5).astype(BF)
        out[rows, CV : CV + HS] = value_grad[rows, :].astype(BF)

        b = proj[rows, CB : CB + NS].astype(BF)
        cc = proj[rows, CC : CC + NS].astype(BF)
        z = proj[rows, CZ : CZ + HW].astype(F32)
        u = proj[rows, CU : CU + HW].astype(F32)
        pre, dt, log_decay = steps(steps_in[rows, :], small)
        cum, decays = block_decays(log_decay)
        last = cum[CH - 1 : CH, :]
        g = dot(cc, b, ((1,), (1,)))
        dt_w = widen(dt)
        v = u * dt_w
        vb = v.astype(BF)
        gated_grad = mix_grad[rows, 0:HW].astype(F32)
        gate = jax.nn.sigmoid(z)
        dy = gated_grad * z * gate
        out[rows, CZ : CZ + HW] = (
            gated_grad * y_in[rows, :] * gate * (1.0 + z * (1.0 - gate))
        ).astype(BF)
        dyb = dy.astype(BF)
        state = states[c]
        sb = state.astype(BF)
        qb = state_grad.astype(BF)
        grow = widen(jnp.exp(cum))
        fade = widen(jnp.exp(last - cum))
        v_grad_inter = fade * dot(b, qb, ((1,), (1,)))
        y_inter = grow * dot(cc, sb, ((1,), (1,)))
        g_grad = jnp.zeros((CH, CH), F32)
        v_grads = []
        cum_grad = jnp.zeros((CH, 8), F32)
        columns = []
        for h in range(HL):
            pair = dot(jnp.where(head_mask(h, (CH, HW)), dyb, jnp.zeros_like(dyb)), vb, ((1,), (1,)))
            mixed_pair = decays[h] * pair
            g_grad = g_grad + mixed_pair
            v_grads.append(dot((decays[h] * g).astype(BF), dyb, ((0,), (0,))))
            swing = mixed_pair * g
            cum_grad = cum_grad + jnp.where(
                lane_ch == h, jnp.sum(swing, axis=1, keepdims=True), 0.0
            )
            columns.append(jnp.sum(swing, axis=0, keepdims=True))
        cum_grad = cum_grad - jnp.concatenate(
            columns + [jnp.zeros((8 - HL, CH), F32)], axis=0
        ).T
        v_grad = per_head(v_grads, (CH, HW)) + v_grad_inter
        g_gradb = g_grad.astype(BF)
        grown = (grow * dy).astype(BF)
        out[rows, CC : CC + NS] = (dot(g_gradb, b) + dot(grown, sb)).astype(BF)
        out[rows, CB : CB + NS] = (
            dot(g_gradb, cc, ((0,), (0,))) + dot((fade * v).astype(BF), qb)
        ).astype(BF)
        out[rows, CU : CU + HW] = (skip_w * dy + dt_w * v_grad).astype(BF)
        both = state * state_grad
        over = jnp.zeros((1, 8), F32)
        for h in range(HL):
            one = jnp.sum(both[h * MP : (h + 1) * MP, :], axis=0, keepdims=True)
            over = over + jnp.where(lane_one == h, jnp.sum(one, axis=1, keepdims=True), 0.0)
        behind = dot((v * v_grad_inter).astype(BF), heads)
        ahead = cum_grad + dot((dy * y_inter).astype(BF), heads)
        decay_grad = (
            dot(ones_low, ahead, ((0,), (0,)), precision=HIGH)
            + dot(ones_low, behind, precision=HIGH)
            - behind
            + jnp.exp(last) * over
        )
        step_grad = dot((u * v_grad).astype(BF), heads) - rate * decay_grad
        r_grad = step_grad * jax.nn.sigmoid(pre)
        out[rows, CR : CR + HS] = jnp.concatenate(
            [r_grad, jnp.zeros((CH, HS - 8), F32)], axis=1
        ).astype(BF)
        acc_bias = acc_bias + jnp.sum(r_grad, axis=0, keepdims=True)
        acc_decay = acc_decay - rate * jnp.sum(dt * decay_grad, axis=0, keepdims=True)
        acc_skip = acc_skip + jnp.sum(dy * u, axis=0, keepdims=True)
        state_grad = row_heads(jnp.exp(last)) * state_grad + dot(grown, cc, ((0,), (0,)))
    skip_sum = jnp.zeros((1, 8), F32)
    for h in range(HL):
        one = jnp.sum(jnp.where(head_mask(h, (1, HW)), acc_skip, 0.0), axis=1, keepdims=True)
        skip_sum = skip_sum + jnp.where(lane_one == h, one, 0.0)
    sums[...] = jnp.concatenate([acc_bias, acc_decay, skip_sum, jnp.zeros((5, 8), F32)], axis=0)


VMEM = pl.BlockSpec(memory_space=pltpu.VMEM)
def cost(us):
    return pl.CostEstimate(flops=int(us * 1e9), bytes_accessed=1 << 20, transcendentals=0)


def params(mib):
    return pltpu.CompilerParams(vmem_limit_bytes=mib * 1024 * 1024)


SMEM = pl.BlockSpec(memory_space=pltpu.SMEM)


def mixer_forward(where, small, out_w, shares, pieces):
    shape = jax.ShapeDtypeStruct
    return pl.pallas_call(
        mixer_forward_kernel,
        out_shape=(
            shape((TOK, D), BF),
            shape((D, CW), BF),
            shape((D, 2 * FL), BF),
            shape((TOK, CW), BF),
            shape((TOK, 8), F32),
            shape((TOK, HW + HS), BF),
            shape((TOK, HW), F32),
            shape((NCH, HW, NS), F32),
            shape((TOK, 8), F32),
            shape((TOK, D), BF),
        ),
        in_specs=[SMEM] + [VMEM] * 19,
        out_specs=(VMEM,) * 10,
        scratch_shapes=[pltpu.VMEM((TOK, HS), BF), pltpu.VMEM((TOK, HS), BF), pltpu.VMEM((CH, CW), F32)],
        cost_estimate=cost(16),
        compiler_params=params(50),
    )(where, small, out_w, *shares, *pieces)


def feed_forward_kernel(*refs):
    where, gu_w, act_grad, *pieces, unit, act, up_grad, e_part = refs
    for piece, place in zip(pieces, PLACES):
        unit[pl.ds(piece_row(where[0], place), piece.shape[0]), :] = piece[...]
    for c in range(NCH):
        rows = slice(c * CH, (c + 1) * CH)
        gate_rows = dot(unit[rows, :], gu_w[...])
        gate, wide = gate_rows[:, :FL], gate_rows[:, FL:]
        s = jax.nn.sigmoid(gate)
        act[rows, :] = (gate * s * wide).astype(BF)
        grad = act_grad[rows, :].astype(F32)
        up_grad[rows, :FL] = (grad * wide * s * (1.0 + gate * (1.0 - s))).astype(BF)
        up_grad[rows, FL:] = (grad * gate * s).astype(BF)
        e_part[rows, :] = dot(up_grad[rows, :], gu_w[...], ((1,), (1,))).astype(BF)


def feed_forward(where, gu_w, act_grad, pieces):
    shape = jax.ShapeDtypeStruct
    return pl.pallas_call(
        feed_forward_kernel,
        out_shape=(
            shape((TOK, D), BF), shape((TOK, FL), BF), shape((TOK, 2 * FL), BF), shape((TOK, D), BF),
        ),
        in_specs=[SMEM] + [VMEM] * 12,
        out_specs=(VMEM,) * 4,
        cost_estimate=cost(6),
        compiler_params=params(50),
    )(where, gu_w, act_grad, *pieces)


def output_gradients_kernel(*refs):
    where, down_w, *pieces, ffn_grad, act_grad = refs
    for piece, place in zip(pieces, PLACES):
        ffn_grad[pl.ds(piece_row(where[0], place), piece.shape[0]), :] = piece[:, D:]
    for c in range(NCH):
        rows = slice(c * CH, (c + 1) * CH)
        act_grad[rows, :] = dot(ffn_grad[rows, :], down_w[...], ((1,), (1,))).astype(BF)


def output_gradients(where, down_w, pieces):
    shape = jax.ShapeDtypeStruct
    return pl.pallas_call(
        output_gradients_kernel,
        out_shape=(shape((TOK, D), BF), shape((TOK, FL), BF)),
        in_specs=[SMEM] + [VMEM] * 10,
        out_specs=(VMEM,) * 2,
        cost_estimate=cost(3),
        compiler_params=params(50),
    )(where, down_w, *pieces)


def branch_kernel(*refs):
    where, out_w, mix, *pieces, mix_grad, out_grad, branch = refs
    for piece, place in zip(pieces, PLACES):
        branch[pl.ds(piece_row(where[0], place), piece.shape[0]), :] = piece[...]
    for c in range(NCH):
        rows = slice(c * CH, (c + 1) * CH)
        mix_grad[rows, :] = dot(branch[rows, :], out_w[...], ((1,), (1,))).astype(BF)
    out_grad[...] = dot(mix[...], branch[...], ((0,), (0,))).astype(BF)


def branch_products(where, out_w, mix, pieces):
    shape = jax.ShapeDtypeStruct
    return pl.pallas_call(
        branch_kernel,
        out_shape=(shape((TOK, HW + HS), BF), shape((HW + HS, D), BF)),
        in_specs=[SMEM] + [VMEM] * 12,
        out_specs=(VMEM,) * 2,
        scratch_shapes=[pltpu.VMEM((TOK, D), BF)],
        cost_estimate=cost(3),
        compiler_params=params(50),
    )(where, out_w, mix, *pieces)


def mixer_backward(proj, step_rows, small, y, states, log_totals, mix_grad):
    return pl.pallas_call(
        mixer_backward_kernel,
        out_shape=(jax.ShapeDtypeStruct((TOK, CW), BF), jax.ShapeDtypeStruct((8, 8), F32)),
        in_specs=[VMEM] * 7,
        out_specs=(VMEM,) * 2,
        scratch_shapes=[
            pltpu.VMEM((TOK, HS), BF),
            pltpu.VMEM((TOK, HS), BF),
            pltpu.VMEM((TOK, HS), F32),
            pltpu.VMEM((TOK, HS), F32),
        ],
        cost_estimate=cost(19),
        compiler_params=params(50),
    )(proj, step_rows, small, y, states, log_totals, mix_grad)


def pack_weights_kernel(where, mixer_w, attn_w, gate_up, gains, out):
    rows = pl.ds(pl.multiple_of(where[2] * 32 + where[1] * 16, 16), 16)
    g1, g2 = gains[rows, 0:1], gains[rows, 1:2]
    lane = lax.broadcasted_iota(jnp.int32, (MH, HS), 1)
    sub = lax.broadcasted_iota(jnp.int32, (MH, HS), 0)

    def part(ref, at, width, g):
        return (ref[rows, at : at + width].astype(F32) * g).astype(BF)

    both = part(mixer_w, 2 * INNER, 2 * NS, g1)
    steps_w = part(mixer_w, 2 * INNER + 2 * NS, MH, g1)
    for s in range(SEQ):
        head = s // (SEQ // KVH) * HS
        out[s, :, CB : CB + 2 * NS] = both
        out[s, :, CZ : CZ + HW] = part(mixer_w, s * HW, HW, g1)
        out[s, :, CQ : CQ + HS] = part(attn_w, s * HS, HS, g1)
        out[s, :, CU : CU + HW] = part(mixer_w, INNER + s * HW, HW, g1)
        out[s, :, CK : CK + HS] = part(attn_w, QH * HS + head, HS, g1)
        out[s, :, CV : CV + HS] = part(attn_w, (QH + KVH) * HS + head, HS, g1)
        own = ((sub == s * HL + lane) & (lane < HL)).astype(BF)
        out[s, :, CR:CW] = dot(steps_w, own).astype(BF)
        out[s, :, CW : CW + FL] = part(gate_up, s * FL, FL, g2)
        out[s, :, CW + FL :] = part(gate_up, FF + s * FL, FL, g2)


def pack_weights(where, mixer_w, attn_w, gate_up, gains):
    return pl.pallas_call(
        pack_weights_kernel,
        out_shape=jax.ShapeDtypeStruct((SEQ, 16, CW + 2 * FL), BF),
        in_specs=[SMEM] + [VMEM] * 4,
        out_specs=VMEM,
        cost_estimate=cost(1),
        compiler_params=params(50),
    )(where, mixer_w, attn_w, gate_up, gains)


WM = 2 * INNER + 2 * NS + MH
WMP = 3456
WA = (QH + 2 * KVH) * HS


WA0 = WMP
WO0 = WMP + WA
WD0 = WO0 + 2 * FF
WALL = WD0 + 4 * D


def mixer_rows_kernel(got, got_gu, thin, out, rows):
    thin_rows = thin[...].astype(F32)
    for k in range(4):
        rows[:, WD0 + k * D : WD0 + (k + 1) * D] = thin_rows[k * 8 : (k + 1) * 8, :]
    for s in range(SEQ):
        rows[:, WO0 + s * 2 * FL : WO0 + (s + 1) * 2 * FL] = sum(
            got_gu[chip * SEQ + s].astype(F32) for chip in range(8)
        )
    share = [sum(got[chip * SEQ + s].astype(F32) for chip in range(8)) for s in range(SEQ)]
    lane = lax.broadcasted_iota(jnp.int32, (16, 128), 1)
    sub = lax.broadcasted_iota(jnp.int32, (16, 128), 0)
    tail = jnp.zeros((8, 128), F32)
    every = sum(share)
    for s in range(SEQ):
        rows[:, s * HW : (s + 1) * HW] = share[s][:, CZ : CZ + HW]
        rows[:, INNER + s * HW : INNER + (s + 1) * HW] = share[s][:, CU : CU + HW]
        rows[:, WA0 + s * HS : WA0 + (s + 1) * HS] = share[s][:, CQ : CQ + HS]
        place = ((lane == s * HL + sub) & (sub < HL)).astype(F32)
        tail = tail + dot(share[s][:, CR : CR + 16], place, precision=HIGH)
    rows[:, 2 * INNER : 2 * INNER + 2 * NS] = every[:, : 2 * NS]
    place = ((lane == MH - 8 + sub) & (sub >= 8)).astype(F32)
    tail = tail + dot(every[:, CR : CR + 16], place, precision=HIGH)
    place = ((lane == MH + 8 + sub) & (sub == 0)).astype(F32)
    tail = tail + dot(every[:, CR + 16 : CR + 32], place, precision=HIGH)
    rows[:, 2 * INNER + 2 * NS : WMP] = tail
    each = SEQ // KVH
    for j in range(KVH):
        both = sum(share[j * each : (j + 1) * each])
        at = WA0 + QH * HS + j * HS
        rows[:, at : at + HS] = both[:, CK : CK + HS]
        at = at + KVH * HS
        rows[:, at : at + HS] = both[:, CV : CV + HS]
    out[...] = rows[...].astype(BF)


def mixer_rows(got, got_gu, thin):
    return pl.pallas_call(
        mixer_rows_kernel,
        out_shape=jax.ShapeDtypeStruct((8, WALL), BF),
        in_specs=[VMEM] * 3,
        out_specs=VMEM,
        scratch_shapes=[pltpu.VMEM((8, WALL), F32)],
        cost_estimate=cost(1),
        compiler_params=params(16),
    )(got, got_gu, thin)


def finish_kernel(
    where, mixer_w, attn_w, gate_up, gains, *refs,
):
    blocks = refs[:8]
    (
    mixer_out, attn_out, gate_up_out, down_out, mamba_rows, attn_rows, gain, line, rows, thin,
    ) = refs[8:]
    core, y, high = where[1], where[2], where[3]
    half = ROWS // 2
    for n, block in enumerate(blocks):
        block = block[...].astype(F32)
        from_core, from_y = (core if n < 4 else 1 - core), (y + n) % 4
        for part in range(2):
            from_high = high if part == 0 else 1 - high
            source = block[part * 8 : (part + 1) * 8, :]
            to = pl.multiple_of(from_core * half + from_y * 16 + from_high * 8, 8)
            rows[pl.ds(to, 8), :] = source[:, :WD0]
            first = from_core * FL + from_y * 64 + from_high * 32
            for k in range(4):
                to = pl.multiple_of(first + k * 8, 8)
                thin[pl.ds(to, 8), :] = source[:, WD0 + k * D : WD0 + (k + 1) * D]
    down_out[...] = thin[:FL, :]
    mamba_rows[...] = thin[FL : FL + HW, :]
    attn_rows[...] = thin[FL + HW :, :]
    line[...] = rows[0:8, WM - MH : WMP] + rows[half : half + 8, WM - MH : WMP]
    for i in range(ROWS // 16):
        at = slice(i * 16, (i + 1) * 16)
        mixer, attn, g = rows[at, :WM], rows[at, WA0:WO0], gains[at, :]
        total = jnp.sum(mixer * mixer_w[at, :].astype(F32), axis=1, keepdims=True) + jnp.sum(
            attn * attn_w[at, :].astype(F32), axis=1, keepdims=True
        )
        rows[at, :WM] = mixer * g[:, 0:1]
        attn_out[at, :] = attn * g[:, 0:1]
        total_two = jnp.zeros((16, 1), F32)
        for s in range(SEQ):
            for k in range(2):
                block = rows[at, WO0 + (s * 2 + k) * FL : WO0 + (s * 2 + k + 1) * FL]
                to = slice(k * FF + s * FL, k * FF + (s + 1) * FL)
                total_two = total_two + jnp.sum(
                    block * gate_up[at, to].astype(F32), axis=1, keepdims=True
                )
                gate_up_out[at, to] = block * g[:, 1:2]
        gain[at, :] = jnp.concatenate([total, total_two], axis=1)
    for i in range(WMP // 128):
        n = min(128, WM - i * 128)
        mixer_out[i * 128 : i * 128 + n, :] = rows[:, i * 128 : (i + 1) * 128].T[:n, :]


def finish(where, mixer_w, attn_w, gate_up, gains, blocks):
    shape = lambda *dims: jax.ShapeDtypeStruct(dims, F32)
    return pl.pallas_call(
        finish_kernel,
        out_shape=(
            shape(WM, ROWS), shape(ROWS, WA), shape(ROWS, 2 * FF), shape(FL, D), shape(HW, D), shape(HS, D),
            shape(ROWS, 2), shape(8, 128),
        ),
        in_specs=[SMEM] + [VMEM] * 12,
        out_specs=(VMEM,) * 8,
        scratch_shapes=[pltpu.VMEM((ROWS, WD0), F32), pltpu.VMEM((2 * FL, D), F32)],
        cost_estimate=cost(6),
        compiler_params=params(32),
    )(where, mixer_w, attn_w, gate_up, gains, *blocks)


def unit_back(x, e):
    rho = lax.rsqrt(jnp.mean(x * x, axis=-1, keepdims=True) + EPS)
    return rho * e - x * (rho * rho * rho) * jnp.mean(x * e, axis=-1, keepdims=True)


def arrived(got, rows):
    return sum(got[k, rows, :].astype(F32) for k in range(SEQ))


def over_rows():
    return [slice(i * 16, (i + 1) * 16) for i in range(ROWS // 16)]


def mid_kernel(got, x, mid, unit):
    for rows in over_rows():
        value = x[rows, :].astype(F32) + arrived(got, rows)
        mid[rows, :] = value
        unit[rows, :] = unit_rows(value).astype(BF)


def mid_grad_kernel(got, cot, mid, grad, low):
    for rows in over_rows():
        value = cot[rows, :].astype(F32) + unit_back(mid[rows, :], arrived(got, rows))
        grad[rows, :] = value
        low[rows, :] = value.astype(BF)


def input_grad_kernel(got, x, mid_grad, grad):
    for rows in over_rows():
        grad[rows, :] = mid_grad[rows, :] + unit_back(x[rows, :].astype(F32), arrived(got, rows))


def output_kernel(got, mid, out):
    for rows in over_rows():
        out[rows, :] = (mid[rows, :] + arrived(got, rows)).astype(BF)


def on_rows(kernel, kinds, *arrays):
    return pl.pallas_call(
        kernel,
        out_shape=tuple(jax.ShapeDtypeStruct((ROWS, D), kind) for kind in kinds),
        in_specs=[VMEM] * len(arrays),
        out_specs=(VMEM,) * len(kinds),
        cost_estimate=cost(2),
        compiler_params=params(16),
    )(*arrays)


def core_sum(grad, core):
    n = grad.shape[1]
    parts = grad.reshape(SEQ, 2, ROWS // 2, n)
    mine = lax.dynamic_index_in_dim(parts, core, 1, False).astype(F32)
    other = core_swap(lax.dynamic_index_in_dim(parts, 1 - core, 1, False))
    both = mine + other.astype(F32)
    return both.astype(BF).reshape(SEQ, 8, 8, n).swapaxes(0, 1).reshape(64, 8, n)


def core_sum_kernel(where, mine, other, line, out):
    first = lax.broadcasted_iota(jnp.int32, (ROWS // 2, CW), 0) == 0
    for j in range(SEQ):
        value = mine[j].astype(F32) + other[j].astype(F32)
        value = value + jnp.where(first & (where[0] == j), line[0:1, :], 0.0)
        for chip in range(8):
            out[chip * SEQ + j] = value[chip * 8 : (chip + 1) * 8, :].astype(BF)


def core_sum_with(where, in_grad, line, core):
    parts = in_grad.reshape(SEQ, 2, ROWS // 2, CW)
    other = core_swap(lax.dynamic_index_in_dim(parts, 1 - core, 1, False))
    mine = lax.dynamic_index_in_dim(parts, core, 1, False)
    return pl.pallas_call(
        core_sum_kernel,
        out_shape=jax.ShapeDtypeStruct((64, 8, CW), BF),
        in_specs=[SMEM] + [VMEM] * 3,
        out_specs=VMEM,
        cost_estimate=cost(1),
        compiler_params=params(16),
    )(where, mine, other, line)


def halved(v, mine, bit):
    v = v.reshape(2, v.shape[0] // 2, v.shape[1])
    other = lax.dynamic_index_in_dim(v, 1 - mine, 0, False)
    other = lax.ppermute(other, "dp", [(i, i ^ bit) for i in range(DP)])
    own = lax.dynamic_index_in_dim(v, mine, 0, False)
    return (own.astype(F32) + other.astype(F32)).astype(BF)


def to_owners(sent):
    return lax.all_to_all(
        sent, ("dp", "seq"), split_axis=0, concat_axis=0, tiled=True, axis_index_groups=same_core()
    )


def local(
    inputs, cotangent, mixer_in, attn_in, mamba_out, attn_out, gate_up, down_proj,
    norm_gains, step_bias, decay_log, skip_gain,
):
    me = lax.axis_index("seq")
    group = lax.axis_index("dp")
    core = group % 2
    high = group // 2 % 2
    where = jnp.stack([me, core, group // 4, high]).astype(jnp.int32)
    x0 = inputs[0]
    gains = norm_gains[0].astype(F32).T
    down_w = down_proj[0]
    out_w = jnp.concatenate([mamba_out[0], attn_out[0]], axis=0)
    small = jnp.concatenate([step_bias, decay_log, skip_gain], axis=0).astype(F32)
    small = jnp.pad(small, ((0, 5), (0, 8 - HL)))

    packed = pack_weights(where, mixer_in[0], attn_in[0], gate_up[0], gains)
    pieces, shares = gather_with_weights(jnp.concatenate([x0, cotangent[0]], axis=1), packed)
    unit_one, in_w, gu_w, proj, step_rows, mix, y, states, log_totals, mid_part = mixer_forward(
        where, small, out_w, shares, pieces
    )
    ffn_grad, act_grad = output_gradients(where, down_w, pieces)
    got, ffn_grad, act_grad = scatter_rows(mid_part, (ffn_grad, act_grad))
    mid, unit_mid = on_rows(mid_kernel, (F32, BF), got, x0)

    unit_two, act, up_grad, e_part = feed_forward(
        where, gu_w, act_grad, gather_pieces(unit_mid)
    )
    gu_sent = core_sum(dot(unit_two, up_grad, ((0,), (0,))).astype(BF), core)
    down_grad = dot(act, ffn_grad, ((0,), (0,))).astype(BF)
    got, gu_sent, out_part, down_grad = scatter_rows(
        e_part, (gu_sent, dot(act, down_w).astype(BF), down_grad)
    )
    mid_grad, branch = on_rows(mid_grad_kernel, (F32, BF), got, cotangent[0], mid)
    pieces = gather_pieces(branch)
    *pieces, gu_got = lax.optimization_barrier((*pieces, to_owners(gu_sent)))

    mix_grad, out_grad = branch_products(where, out_w, mix, pieces)
    kept = core_swap(jnp.where(core == 0, out_grad, down_grad))
    mix_grad, out_part = lax.optimization_barrier((mix_grad, out_part))
    thin = jnp.where(core == 0, down_grad, out_grad).astype(F32) + kept.astype(F32)
    mix_grad, thin = lax.optimization_barrier((mix_grad, thin.astype(BF)))
    proj_grad, sums = mixer_backward(proj, step_rows, small, y, states, log_totals, mix_grad)
    proj_grad, thin = lax.optimization_barrier((proj_grad, halved(thin, group // 8, 8)))
    in_grad = dot(unit_one, proj_grad, ((0,), (0,))).astype(BF)
    line = jnp.concatenate([sums[0, :HL], sums[1, :HL], sums[2, :HL]])
    line = jnp.pad(line, (CR + 8, CW - CR - 8 - 3 * HL))
    line = jnp.broadcast_to(line[None], (8, CW))
    result, sent = scatter_rows(out_part, (core_sum_with(where, in_grad, line, core),))
    (outputs,) = on_rows(output_kernel, (BF,), result, mid)
    sent, proj_grad, thin = lax.optimization_barrier((sent, proj_grad, thin))
    e_part = dot(proj_grad, in_w, ((1,), (1,))).astype(BF)
    e_part, thin = lax.optimization_barrier((e_part, halved(thin, group // 4 % 2, 4)))
    thin = halved(thin, high, 2)
    got, outputs = lax.optimization_barrier((to_owners(sent), outputs))
    rows = mixer_rows(got, gu_got, thin)
    rows, e_part = lax.optimization_barrier((rows, e_part))
    other_rows = lax.ppermute(rows, "dp", [(i, i ^ 2) for i in range(DP)])
    blocks = round_y(jnp.concatenate([rows, other_rows], axis=0))
    blocks = (*blocks, *(core_swap(v) for v in blocks))
    (got,) = scatter_rows(e_part)
    (input_grad,) = on_rows(input_grad_kernel, (F32,), got, x0, mid_grad)
    mixer_g, attn_g, gate_up_g, down_g, mamba_out_g, attn_out_g, gain, line = finish(
        where, mixer_in[0], attn_in[0], gate_up[0], gains, blocks
    )
    line = line[0:1, MH : MH + 3 * HL]
    return (
        outputs[None],
        input_grad[None],
        mixer_g.T[None],
        attn_g[None],
        mamba_out_g[None],
        attn_out_g[None],
        gate_up_g[None],
        down_g[None],
        gain.T[None],
        line[:, :HL],
        line[:, HL : 2 * HL],
        line[:, 2 * HL :],
    )


def solution(mesh):
    rows = P("dp", "seq", None)
    owned = P(None, "seq", None)
    heads = P(None, "seq")
    gains = P(None, None, "seq")
    return jax.shard_map(
        local,
        mesh=mesh,
        in_specs=(rows, rows) + (owned,) * 6 + (gains,) + (heads,) * 3,
        out_specs=(rows, rows) + (owned,) * 6 + (gains,) + (heads,) * 3,
        check_vma=False,
    )
```
